256 devices in a mesh: dp: 16 (over z, core), expert: 16 (over y, x).
Axes of the slice: x: 4, y: 4, z: 8, core: 2. Of those that a mesh axis runs over, the one named last changes fastest.
Arguments:
- grad: float32 [16, 2048, 1408], P('expert', 'dp'), may hold values from -700 to 700
- expert_ids: int32 [16], replicated, may hold values from 0 to 15, each once
Outputs:
- update: bfloat16 [16, 2048, 1408], P('expert', 'dp')
The draws below stay inside these ranges and needn't reach their ends.
Inputs may be any that keep to these rules, and one draw needn't show every extreme that they name: `expert_ids`: each of the 16 numbers appears once.
All inputs are finite; a program needn't handle non-finite values.
Results may differ from the reference program's by a relative error of at most 0.0065.
Values may be sent and summed in bfloat16 or wider, within the bound.
A program may use at most 64 MiB of HBM per device.

```python
import math
import jax
import jax.numpy as jnp
from jax import lax

D = 2048
F = 1408
MATS = 16
ITERS = 2
R = 128
RQ = 8
N_EXPERT = 16


def draw_grad(key, part):
    key = jax.random.fold_in(key, 11)
    key_rows, key_columns, key_noise = jax.random.split(key, 3)
    row_index = jnp.arange(D)
    rising = jnp.sqrt(1.0 + 2.0 * (row_index % R // RQ).astype(jnp.float32) / max(N_EXPERT - 1, 1))
    row_scale = jnp.exp(jax.random.uniform(key_rows, (MATS, D), minval=0.0, maxval=math.log(10.0))) * rising[None, :]
    column_scale = jnp.exp(jax.random.uniform(key_columns, (MATS, F), minval=0.0, maxval=math.log(10.0)))
    noise_part = jnp.clip(jax.random.normal(key_noise, (MATS, D, F)), -4.0, 4.0)
    return (noise_part * row_scale[:, :, None] * column_scale[:, None, :]).astype(jnp.float32)


def setup_inputs(seed: int = 0) -> dict:
    keys = jax.random.split(jax.random.key(seed), 3)
    grad = draw_grad(jax.random.fold_in(keys[2], 71), 0)
    expert_ids = jax.random.permutation(keys[1], MATS).astype(jnp.int32)
    return {"grad": grad, "expert_ids": expert_ids}


coef_a = 3.4445
coef_b = -4.775
coef_c = 2.0315
gram_eps = 1e-07

def newton_update(grad_one):
    current = grad_one.astype(jnp.bfloat16)
    mixed = current.astype(jnp.float32)
    for iteration in range(ITERS):
        gram_raw = jnp.dot(current.T, current, preferred_element_type=jnp.float32)
        if iteration == 0:
            norm_value = jnp.sqrt(jnp.sum(gram_raw * gram_raw)) + gram_eps
            inverse = 1.0 / norm_value
            row_factor = 1.0 / jnp.sqrt(norm_value)
        else:
            inverse = jnp.float32(1.0)
            row_factor = jnp.float32(1.0)
        gram = (gram_raw * inverse).astype(jnp.bfloat16)
        square = jnp.dot(gram, gram, preferred_element_type=jnp.float32)
        poly = (coef_b * gram.astype(jnp.float32) + coef_c * square).astype(jnp.bfloat16)
        product = jnp.dot(current, poly, preferred_element_type=jnp.float32)
        mixed = row_factor * (coef_a * current.astype(jnp.float32) + product)
        if iteration < ITERS - 1:
            current = mixed.astype(jnp.bfloat16)
    return (math.sqrt(max(D, F)) * mixed).astype(jnp.bfloat16)

def reference(grad, expert_ids):
    results = lax.map(newton_update, grad)
    update = jnp.zeros((MATS, D, F), jnp.bfloat16)
    return update.at[expert_ids.astype(jnp.int32)].set(results)
```

```python
import math

import jax
import jax.numpy as jnp
from jax import lax
from jax.experimental import pallas as pl
from jax.experimental.pallas import tpu as pltpu
from jax.sharding import PartitionSpec as P

D = 2048
F = 1408
ROWS = 128
GROUP = 16
GROUPS = 8
TEAM = 16
RING = 8
STEPS = 8

coef_a = 3.4445
coef_b = -4.775
coef_c = 2.0315
gram_eps = 1e-07

MESH = pl.DeviceIdType.MESH
PANELS = [(i, min(256, F - i)) for i in range(0, F, 256)]


def kernel(
    grad_ref,
    ids_ref,
    out_ref,
    own,
    mid,
    stage,
    slots,
    turned,
    gram,
    amat,
    base,
    once,
    total,
    first,
    send1,
    recv1,
    send2,
    recv2,
    send_up,
    recv_up,
    send_down,
    recv_down,
    send_sib,
    recv_sib,
):
    dp = lax.axis_index("dp")
    me = lax.axis_index("expert")
    core = lax.rem(dp, 2)
    z = dp // 2
    sib = dp + 1 - 2 * core
    up = lax.rem(z + 1, RING) * 2 + core
    down = lax.rem(z + RING - 1, RING) * 2 + core

    barrier = pltpu.get_barrier_semaphore()
    for k in range(1, TEAM):
        pl.semaphore_signal(
            barrier, inc=1, device_id=(dp, lax.rem(me + k, TEAM)), device_id_type=MESH
        )
    for other in (sib, up, down):
        pl.semaphore_signal(barrier, inc=1, device_id=(other, me), device_id_type=MESH)
    own[...] = grad_ref[...].reshape(GROUPS, GROUP, F).astype(jnp.bfloat16)
    pl.semaphore_wait(barrier, TEAM + 2)

    def copy1(g):
        return pltpu.make_async_remote_copy(
            src_ref=own.at[g],
            dst_ref=mid.at[me],
            send_sem=send1.at[g],
            recv_sem=recv1.at[me],
            device_id=(dp, 2 * g + core),
            device_id_type=MESH,
        )

    def arrive1(s):
        return pltpu.make_async_remote_copy(
            src_ref=own.at[0],
            dst_ref=mid.at[s],
            send_sem=send1.at[0],
            recv_sem=recv1.at[s],
            device_id=(dp, s),
            device_id_type=MESH,
        )

    def copy2(e, g):
        return pltpu.make_async_remote_copy(
            src_ref=stage.at[e],
            dst_ref=slots.at[0, g],
            send_sem=send2.at[e],
            recv_sem=recv2.at[g],
            device_id=(dp, e),
            device_id_type=MESH,
        )

    def arrive2(g):
        return pltpu.make_async_remote_copy(
            src_ref=stage.at[0],
            dst_ref=slots.at[0, g],
            send_sem=send2.at[0],
            recv_sem=recv2.at[g],
            device_id=(dp, 2 * g + core),
            device_id_type=MESH,
        )

    my_group = me // 2
    relay = lax.rem(me, 2) == core

    @pl.loop(0, GROUPS)
    def _(g):
        @pl.when(2 * g + core != me)
        def _():
            copy1(g).start()

    @pl.when(relay)
    def _():
        mid[me] = own[my_group]

    gram[...] = jnp.zeros_like(gram)

    @pl.when(relay)
    def _():
        @pl.loop(0, TEAM)
        def _(s):
            @pl.when(s != me)
            def _():
                arrive1(s).wait_recv()

        @pl.loop(0, TEAM)
        def _(k):
            e = lax.rem(me + k, TEAM)
            slot = jnp.int32(0)
            for j in range(TEAM):
                slot = jnp.where(ids_ref[j] == e, j, slot)
            stage[e] = mid[slot]

            @pl.when(e == me)
            def _():
                slots[0, my_group] = stage[e]

            @pl.when(e != me)
            def _():
                copy2(e, my_group).start()

    @pl.loop(0, GROUPS)
    def _(g):
        @pl.when(2 * g + core != me)
        def _():
            arrive2(g).wait_recv()

    half = GROUPS // 2
    lower, upper = pl.ds(0, half), pl.ds(half, half)

    def copy_up(src, part, t):
        return pltpu.make_async_remote_copy(
            src_ref=slots.at[src, part],
            dst_ref=slots.at[t, lower],
            send_sem=send_up.at[t],
            recv_sem=recv_up.at[t],
            device_id=(up, me),
            device_id_type=MESH,
        )

    def copy_down(src, part, t):
        return pltpu.make_async_remote_copy(
            src_ref=slots.at[src, part],
            dst_ref=slots.at[t, upper],
            send_sem=send_down.at[t],
            recv_sem=recv_down.at[t],
            device_id=(down, me),
            device_id_type=MESH,
        )

    def copy_sib(t):
        return pltpu.make_async_remote_copy(
            src_ref=slots.at[t, pl.ds(0, GROUPS)],
            dst_ref=slots.at[t, pl.ds(GROUPS, GROUPS)],
            send_sem=send_sib.at[t],
            recv_sem=recv_sib.at[t],
            device_id=(sib, me),
            device_id_type=MESH,
        )

    copy_up(0, lower, 1).start()
    copy_down(0, upper, 1).start()
    copy_up(0, upper, 2).start()
    copy_down(0, lower, 2).start()

    @pl.loop(0, STEPS)
    def _(t):
        @pl.when(t > 0)
        def _():
            copy_up(t, lower, t).wait_recv()
            copy_down(t, upper, t).wait_recv()

            @pl.when(t + 2 < STEPS)
            def _():
                copy_up(t, lower, t + 2).start()
                copy_down(t, upper, t + 2).start()

        copy_sib(t).start()
        copy_sib(t).wait_recv()
        rows = slots[t].reshape(2 * ROWS, F)
        turned[...] = rows.T
        for start, size in PANELS:
            gram[:, start : start + size] += jnp.dot(
                turned[...],
                slots[t, :, :, start : start + size].reshape(2 * ROWS, size),
                preferred_element_type=jnp.float32,
            )

    def square(i, acc):
        g = gram[pl.ds(pl.multiple_of(i * 128, 128), 128), :]
        return acc + jnp.sum((g * g).reshape(16, 8, F), axis=0)

    squares = lax.fori_loop(0, F // 128, square, jnp.zeros((8, F), jnp.float32))
    norm = jnp.sqrt(jnp.sum(squares, keepdims=True).reshape(1, 1)) + gram_eps
    inverse = 1.0 / norm
    factor = 1.0 / jnp.sqrt(norm)

    @pl.loop(0, F // 128)
    def _(i):
        part = pl.ds(pl.multiple_of(i * 128, 128), 128)
        amat[part, :] = (gram[part, :] * inverse).astype(jnp.bfloat16)

    def times(dst, src):
        x = src[...].astype(jnp.bfloat16)
        for start, size in PANELS:
            dst[:, start : start + size] = jnp.dot(
                x, amat[:, start : start + size], preferred_element_type=jnp.float32
            )

    def poly():
        times(once, base)
        base[...] = coef_a * base[...] + coef_b * once[...]
        x = once[...].astype(jnp.bfloat16)
        for start, size in PANELS:
            base[:, start : start + size] += coef_c * jnp.dot(
                x, amat[:, start : start + size], preferred_element_type=jnp.float32
            )

    base[...] = slots[0, 0:GROUPS].reshape(ROWS, F).astype(jnp.float32)
    poly()
    first[...] = (factor * base[...]).astype(jnp.bfloat16)
    base[...] = first[...].astype(jnp.float32)
    total[...] = coef_a * base[...]

    @pl.loop(0, 2)
    def _(it):
        poly()
        times(once, base)
        base[...] = once[...]
        poly()
        total[...] += jnp.where(it == 0, coef_b, coef_c) * base[...]

    out_ref[...] = (math.sqrt(max(D, F)) * total[...]).astype(jnp.bfloat16)

    @pl.loop(0, GROUPS)
    def _(g):
        @pl.when(2 * g + core != me)
        def _():
            copy1(g).wait_send()

    @pl.when(relay)
    def _():
        @pl.loop(0, TEAM)
        def _(e):
            @pl.when(e != me)
            def _():
                copy2(e, my_group).wait_send()

    @pl.loop(0, STEPS)
    def _(t):
        copy_sib(t).wait_send()

        @pl.when(t > 0)
        def _():
            copy_up(t, lower, t).wait_send()
            copy_down(t, upper, t).wait_send()


def body(grad, expert_ids):
    dma = pltpu.SemaphoreType.DMA
    bf16, f32 = jnp.bfloat16, jnp.float32
    out = pl.pallas_call(
        kernel,
        out_shape=jax.ShapeDtypeStruct((ROWS, F), bf16),
        in_specs=[
            pl.BlockSpec(memory_space=pltpu.VMEM),
            pl.BlockSpec(memory_space=pltpu.SMEM),
        ],
        out_specs=pl.BlockSpec(memory_space=pltpu.VMEM),
        scratch_shapes=[
            pltpu.VMEM((GROUPS, GROUP, F), bf16),
            pltpu.VMEM((TEAM, GROUP, F), bf16),
            pltpu.VMEM((TEAM, GROUP, F), bf16),
            pltpu.VMEM((STEPS, 2 * GROUPS, GROUP, F), bf16),
            pltpu.VMEM((F, 2 * ROWS), bf16),
            pltpu.VMEM((F, F), f32),
            pltpu.VMEM((F, F), bf16),
            pltpu.VMEM((ROWS, F), f32),
            pltpu.VMEM((ROWS, F), f32),
            pltpu.VMEM((ROWS, F), f32),
            pltpu.VMEM((ROWS, F), bf16),
            dma((GROUPS,)),
            dma((TEAM,)),
            dma((TEAM,)),
            dma((GROUPS,)),
            dma((STEPS,)),
            dma((STEPS,)),
            dma((STEPS,)),
            dma((STEPS,)),
            dma((STEPS,)),
            dma((STEPS,)),
        ],
        compiler_params=pltpu.CompilerParams(
            collective_id=0,
            has_side_effects=True,
            vmem_limit_bytes=48 * 1024 * 1024,
        ),
        cost_estimate=pl.CostEstimate(
            flops=2 * F * F * (D + 12 * ROWS), bytes_accessed=6 * ROWS * F, transcendentals=0
        ),
    )(grad.reshape(ROWS, F), expert_ids)
    return out.reshape(1, ROWS, F)


def solution(mesh):
    return jax.shard_map(
        body,
        mesh=mesh,
        in_specs=(P("expert", "dp", None), P()),
        out_specs=P("expert", "dp", None),
        check_vma=False,
    )
```

```python
import math

import jax
import jax.numpy as jnp
from jax import lax
from jax.experimental import pallas as pl
from jax.experimental.pallas import tpu as pltpu
from jax.sharding import PartitionSpec as P

D = 2048
F = 1408
ROWS = 128
GROUP = 16
GROUPS = 8
TEAM = 16
RING = 8
STEPS = 8

coef_a = 3.4445
coef_b = -4.775
coef_c = 2.0315
gram_eps = 1e-07

MESH = pl.DeviceIdType.MESH
SPLIT = [(0, 640), (640, 768)]
PANELS = [(i, min(256, F - i)) for i in range(0, F, 256)]


def kernel(
    grad_ref,
    ids_ref,
    out_ref,
    raw,
    ids,
    holder,
    own,
    mid,
    stage,
    slots,
    turned,
    gram,
    amat,
    base,
    total,
    left,
    right,
    load_raw,
    load_ids,
    send1,
    recv1,
    send2,
    recv2,
    send_up,
    recv_up,
    send_down,
    recv_down,
    send_sib,
    recv_sib,
):
    dp = lax.axis_index("dp")
    me = lax.axis_index("expert")
    core = lax.rem(dp, 2)
    z = dp // 2
    sib = dp + 1 - 2 * core
    up = lax.rem(z + 1, RING) * 2 + core
    down = lax.rem(z + RING - 1, RING) * 2 + core

    fetch_raw = pltpu.make_async_copy(grad_ref, raw, load_raw)
    fetch_ids = pltpu.make_async_copy(ids_ref, ids, load_ids)
    fetch_raw.start()
    fetch_ids.start()
    barrier = pltpu.get_barrier_semaphore()

    @pl.loop(1, TEAM)
    def _(k):
        pl.semaphore_signal(
            barrier, inc=1, device_id=(dp, lax.rem(me + k, TEAM)), device_id_type=MESH
        )

    for other in (sib, up, down):
        pl.semaphore_signal(barrier, inc=1, device_id=(other, me), device_id_type=MESH)
    fetch_raw.wait()
    own[...] = raw[...].reshape(GROUPS, GROUP, F).astype(jnp.bfloat16)
    fetch_ids.wait()

    @pl.loop(0, TEAM)
    def _(e):
        slot = jnp.int32(0)
        for j in range(TEAM):
            slot = jnp.where(ids[j] == e, j, slot)
        holder[e] = slot

    pl.semaphore_wait(barrier, TEAM + 2)

    def relay_of(wave, row, side):
        return 4 * row + 2 * side + lax.rem(row + wave + core, 2)

    my_x, my_y = lax.rem(me, 4), me // 4
    my_group = 4 * lax.rem(my_x + my_y + core, 2) + my_y
    my_side = my_x // 2

    def piece(side):
        return pl.ds(*SPLIT[side])

    def copy1(wave, row, side):
        g = 4 * wave + row
        return pltpu.make_async_remote_copy(
            src_ref=own.at[g, :, piece(side)],
            dst_ref=mid.at[me, :, piece(side)],
            send_sem=send1.at[2 * g + side],
            recv_sem=recv1.at[me],
            device_id=(dp, relay_of(wave, row, side)),
            device_id_type=MESH,
        )

    def arrive1(s, side):
        return pltpu.make_async_remote_copy(
            src_ref=own.at[0, :, piece(side)],
            dst_ref=mid.at[s, :, piece(side)],
            send_sem=send1.at[0],
            recv_sem=recv1.at[s],
            device_id=(dp, s),
            device_id_type=MESH,
        )

    def copy2(e, side):
        return pltpu.make_async_remote_copy(
            src_ref=stage.at[e, :, piece(side)],
            dst_ref=slots.at[0, my_group, :, piece(side)],
            send_sem=send2.at[e],
            recv_sem=recv2.at[2 * my_group + side],
            device_id=(dp, e),
            device_id_type=MESH,
        )

    def arrive2(wave, row, side):
        g = 4 * wave + row
        return pltpu.make_async_remote_copy(
            src_ref=stage.at[0, :, piece(side)],
            dst_ref=slots.at[0, g, :, piece(side)],
            send_sem=send2.at[0],
            recv_sem=recv2.at[2 * g + side],
            device_id=(dp, relay_of(wave, row, side)),
            device_id_type=MESH,
        )

    for wave in range(2):

        @pl.loop(0, 4)
        def _(k):
            row = lax.rem(k + me, 4)
            for side in range(2):

                @pl.when(relay_of(wave, row, side) != me)
                def _():
                    copy1(wave, row, side).start()

    for side in range(2):

        @pl.when(my_side == side)
        def _():
            mid[me, :, piece(side)] = own[my_group, :, piece(side)]

    gram[...] = jnp.zeros_like(gram)

    for side in range(2):

        @pl.when(my_side == side)
        def _():
            @pl.loop(0, TEAM)
            def _(s):
                @pl.when(s != me)
                def _():
                    arrive1(s, side).wait_recv()

            @pl.loop(0, TEAM)
            def _(k):
                e = lax.rem(me + k, TEAM)
                stage[e, :, piece(side)] = mid[holder[e], :, piece(side)]

                @pl.when(e == me)
                def _():
                    slots[0, my_group, :, piece(side)] = stage[e, :, piece(side)]

                @pl.when(e != me)
                def _():
                    copy2(e, side).start()

    def part(first_group, count):
        return pl.ds(first_group, count)

    half = GROUPS // 2
    lower, upper = part(0, half), part(half, half)

    def copy_up(src, src_part, t, dst_part, sem):
        return pltpu.make_async_remote_copy(
            src_ref=slots.at[src, src_part],
            dst_ref=slots.at[t, dst_part],
            send_sem=send_up.at[sem],
            recv_sem=recv_up.at[sem],
            device_id=(up, me),
            device_id_type=MESH,
        )

    def copy_down(src, src_part, t, dst_part, sem):
        return pltpu.make_async_remote_copy(
            src_ref=slots.at[src, src_part],
            dst_ref=slots.at[t, dst_part],
            send_sem=send_down.at[sem],
            recv_sem=recv_down.at[sem],
            device_id=(down, me),
            device_id_type=MESH,
        )

    def copy_sib(t):
        return pltpu.make_async_remote_copy(
            src_ref=slots.at[t, part(0, GROUPS)],
            dst_ref=slots.at[t, part(GROUPS, GROUPS)],
            send_sem=send_sib.at[t],
            recv_sem=recv_sib.at[t],
            device_id=(sib, me),
            device_id_type=MESH,
        )

    def down_piece(src, t, p):
        rows = part(half + 2 * p, 2)
        return copy_down(src, rows, t, rows, STEPS - 2 + 2 * (t - (STEPS - 2)) + p)

    for wave in range(2):

        @pl.loop(0, 4)
        def _(row):
            for side in range(2):

                @pl.when(relay_of(wave, row, side) != me)
                def _():
                    arrive2(wave, row, side).wait_recv()

        sent = part(4 * wave, 4)
        copy_up(0, sent, wave + 1, lower, wave + 1).start()
        copy_down(0, sent, wave + 1, upper, wave + 1).start()

    def turn(t):
        turned[...] = slots[t].reshape(2 * ROWS, F).T

    def columns(t, start, size):
        return slots[t, :, :, start : start + size].reshape(2 * ROWS, size)

    def meet(t):
        copy_sib(t).start()
        copy_sib(t).wait_recv()
        turn(t)

    @pl.loop(0, STEPS - 1)
    def _(t):
        @pl.when(t == STEPS - 2)
        def _():
            for p in range(2):
                down_piece(4, 6, p).wait_recv()
                down_piece(6, 7, p).start()
            copy_up(4, lower, 6, lower, 6).wait_recv()

        @pl.when((t > 0) & (t < STEPS - 2))
        def _():
            copy_up(t, lower, t, lower, t).wait_recv()
            copy_up(t, lower, t + 2, lower, t + 2).start()
            copy_down(t, upper, t, upper, t).wait_recv()

            @pl.when(t < STEPS - 4)
            def _():
                copy_down(t, upper, t + 2, upper, t + 2).start()

            @pl.when(t == STEPS - 4)
            def _():
                for p in range(2):
                    down_piece(4, 6, p).start()

        meet(t)
        for start, size in PANELS:
            end = start + size
            gram[0:end, start:end] += jnp.dot(
                turned[0:end, :], columns(t, start, size), preferred_element_type=jnp.float32
            )

    last = STEPS - 1
    copy_up(5, lower, last, lower, last).wait_recv()
    for p in range(2):
        down_piece(6, last, p).wait_recv()
    meet(last)
    squares = jnp.zeros((8, 128), jnp.float32)
    for start, size in PANELS:
        end = start + size
        panel = columns(last, start, size)
        for row, count in PANELS:
            if row > start:
                break
            rows = slice(row, row + count)
            g = gram[rows, start:end] + jnp.dot(
                turned[rows, :], panel, preferred_element_type=jnp.float32
            )
            amat[rows, start:end] = g.astype(jnp.bfloat16)
            folded = jnp.sum((g * g).reshape(count // 8, 8, size), axis=0)
            for lane in range(0, size, 128):
                lanes = folded[:, lane : lane + 128]
                squares = squares + (lanes if row == start else 2.0 * lanes)
        if start:
            amat[start:end, 0:start] = amat[0:start, start:end].T
    norm = jnp.sqrt(jnp.sum(squares, keepdims=True)) + gram_eps
    inverse = 1.0 / norm
    factor = 1.0 / jnp.sqrt(norm)

    def product(src, finish):
        for start, size in PANELS:
            cols = slice(start, start + size)
            finish(
                cols,
                inverse
                * jnp.dot(src[...], amat[:, cols], preferred_element_type=jnp.float32),
            )

    def poly(src, spare, finish):
        def linear(cols, u):
            base[:, cols] = coef_a * base[:, cols] + coef_b * u
            spare[:, cols] = u.astype(jnp.bfloat16)

        def quadratic(cols, u):
            finish(cols, base[:, cols] + coef_c * u)

        product(src, linear)
        product(spare, quadratic)

    def keep(dst):
        def finish(cols, value):
            base[:, cols] = value
            dst[:, cols] = value.astype(jnp.bfloat16)

        return finish

    def first(cols, value):
        y = (factor * value).astype(jnp.bfloat16)
        left[:, cols] = y
        base[:, cols] = y.astype(jnp.float32)
        total[:, cols] = coef_a * y.astype(jnp.float32)

    def second(cols, value):
        keep(right)(cols, value)
        total[:, cols] += coef_b * value

    def third(cols, value):
        result = total[:, cols] + coef_c * value
        out_ref[:, cols] = (math.sqrt(max(D, F)) * result).astype(jnp.bfloat16)

    left[...] = slots[0, 0:GROUPS].reshape(ROWS, F)
    base[...] = left[...].astype(jnp.float32)
    poly(left, right, first)
    poly(left, right, keep(left))
    product(left, keep(right))
    poly(right, left, second)
    poly(right, left, keep(right))
    product(right, keep(left))
    poly(left, right, third)

    for wave in range(2):

        @pl.loop(0, 4)
        def _(row):
            for side in range(2):

                @pl.when(relay_of(wave, row, side) != me)
                def _():
                    copy1(wave, row, side).wait_send()

    for side in range(2):

        @pl.when(my_side == side)
        def _():
            @pl.loop(0, TEAM)
            def _(e):
                @pl.when(e != me)
                def _():
                    copy2(e, side).wait_send()

    @pl.loop(0, STEPS)
    def _(t):
        copy_sib(t).wait_send()

        @pl.when(t > 0)
        def _():
            copy_up(t, lower, t, lower, t).wait_send()

            @pl.when(t < STEPS - 2)
            def _():
                copy_down(t, upper, t, upper, t).wait_send()

    for p in range(2):
        down_piece(4, 6, p).wait_send()
        down_piece(6, 7, p).wait_send()


def body(grad, expert_ids):
    dma = pltpu.SemaphoreType.DMA
    bf16, f32 = jnp.bfloat16, jnp.float32
    out = pl.pallas_call(
        kernel,
        out_shape=jax.ShapeDtypeStruct((ROWS, F), bf16),
        in_specs=[pl.BlockSpec(memory_space=pl.ANY)] * 2,
        out_specs=pl.BlockSpec(memory_space=pltpu.VMEM),
        scratch_shapes=[
            pltpu.VMEM((ROWS, F), f32),
            pltpu.SMEM((TEAM,), jnp.int32),
            pltpu.SMEM((TEAM,), jnp.int32),
            pltpu.VMEM((GROUPS, GROUP, F), bf16),
            pltpu.VMEM((TEAM, GROUP, F), bf16),
            pltpu.VMEM((TEAM, GROUP, F), bf16),
            pltpu.VMEM((STEPS, 2 * GROUPS, GROUP, F), bf16),
            pltpu.VMEM((F, 2 * ROWS), bf16),
            pltpu.VMEM((F, F), f32),
            pltpu.VMEM((F, F), bf16),
            pltpu.VMEM((ROWS, F), f32),
            pltpu.VMEM((ROWS, F), f32),
            pltpu.VMEM((ROWS, F), bf16),
            pltpu.VMEM((ROWS, F), bf16),
            dma,
            dma,
            dma((2 * GROUPS,)),
            dma((TEAM,)),
            dma((TEAM,)),
            dma((2 * GROUPS,)),
            dma((STEPS,)),
            dma((STEPS,)),
            dma((STEPS + 2,)),
            dma((STEPS + 2,)),
            dma((STEPS,)),
            dma((STEPS,)),
        ],
        compiler_params=pltpu.CompilerParams(
            collective_id=0,
            has_side_effects=True,
            vmem_limit_bytes=55800000,
        ),
        cost_estimate=pl.CostEstimate(
            flops=2 * F * F * (D + 12 * ROWS), bytes_accessed=6 * ROWS * F, transcendentals=0
        ),
    )(grad.reshape(ROWS, F), expert_ids)
    return out.reshape(1, ROWS, F)


def solution(mesh):
    return jax.shard_map(
        body,
        mesh=mesh,
        in_specs=(P("expert", "dp", None), P()),
        out_specs=P("expert", "dp", None),
        check_vma=False,
    )
```

```python
import math

import jax
import jax.numpy as jnp
from jax import lax
from jax.experimental import pallas as pl
from jax.experimental.pallas import tpu as pltpu
from jax.sharding import PartitionSpec as P

D = 2048
F = 1408
ROWS = 128
GROUP = 16
GROUPS = 8
TEAM = 16
RING = 8
STEPS = 8

coef_a = 3.4445
coef_b = -4.775
coef_c = 2.0315
gram_eps = 1e-07

MESH = pl.DeviceIdType.MESH
SPLIT = [(0, 640), (640, 768)]
PANELS = [(i, min(256, F - i)) for i in range(0, F, 256)]


def kernel(
    grad_ref,
    ids_ref,
    out_ref,
    raw,
    ids,
    holder,
    own,
    mid,
    stage,
    slots,
    turned,
    gram,
    amat,
    base,
    total,
    left,
    right,
    load_raw,
    load_ids,
    send1,
    recv1,
    send2,
    recv2,
    send_up,
    recv_up,
    send_down,
    recv_down,
    send_sib,
    recv_sib,
):
    dp = lax.axis_index("dp")
    me = lax.axis_index("expert")
    core = lax.rem(dp, 2)
    z = dp // 2
    sib = dp + 1 - 2 * core
    up = lax.rem(z + 1, RING) * 2 + core
    down = lax.rem(z + RING - 1, RING) * 2 + core

    fetch_raw = pltpu.make_async_copy(grad_ref, raw, load_raw)
    fetch_ids = pltpu.make_async_copy(ids_ref, ids, load_ids)
    fetch_raw.start()
    fetch_ids.start()
    barrier = pltpu.get_barrier_semaphore()

    @pl.loop(1, TEAM)
    def _(k):
        pl.semaphore_signal(
            barrier, inc=1, device_id=(dp, lax.rem(me + k, TEAM)), device_id_type=MESH
        )

    for other in (sib, up, down):
        pl.semaphore_signal(barrier, inc=1, device_id=(other, me), device_id_type=MESH)
    fetch_raw.wait()
    own[...] = raw[...].reshape(GROUPS, GROUP, F).astype(jnp.bfloat16)
    fetch_ids.wait()

    @pl.loop(0, TEAM)
    def _(e):
        slot = jnp.int32(0)
        for j in range(TEAM):
            slot = jnp.where(ids[j] == e, j, slot)
        holder[e] = slot

    pl.semaphore_wait(barrier, TEAM + 2)

    def relay_of(wave, row, side):
        return 4 * row + 2 * side + lax.rem(row + wave + core, 2)

    my_x, my_y = lax.rem(me, 4), me // 4
    my_group = 4 * lax.rem(my_x + my_y + core, 2) + my_y
    my_side = my_x // 2

    def piece(side):
        return pl.ds(*SPLIT[side])

    def copy1(wave, row, side):
        g = 4 * wave + row
        return pltpu.make_async_remote_copy(
            src_ref=own.at[g, :, piece(side)],
            dst_ref=mid.at[me, :, piece(side)],
            send_sem=send1.at[2 * g + side],
            recv_sem=recv1.at[me],
            device_id=(dp, relay_of(wave, row, side)),
            device_id_type=MESH,
        )

    def arrive1(s, side):
        return pltpu.make_async_remote_copy(
            src_ref=own.at[0, :, piece(side)],
            dst_ref=mid.at[s, :, piece(side)],
            send_sem=send1.at[0],
            recv_sem=recv1.at[s],
            device_id=(dp, s),
            device_id_type=MESH,
        )

    def copy2(e, side):
        return pltpu.make_async_remote_copy(
            src_ref=stage.at[e, :, piece(side)],
            dst_ref=slots.at[0, my_group, :, piece(side)],
            send_sem=send2.at[e],
            recv_sem=recv2.at[2 * my_group + side],
            device_id=(dp, e),
            device_id_type=MESH,
        )

    def arrive2(wave, row, side):
        g = 4 * wave + row
        return pltpu.make_async_remote_copy(
            src_ref=stage.at[0, :, piece(side)],
            dst_ref=slots.at[0, g, :, piece(side)],
            send_sem=send2.at[0],
            recv_sem=recv2.at[2 * g + side],
            device_id=(dp, relay_of(wave, row, side)),
            device_id_type=MESH,
        )

    for wave in range(2):

        @pl.loop(0, 4)
        def _(k):
            row = lax.rem(k + me, 4)
            for side in range(2):

                @pl.when(relay_of(wave, row, side) != me)
                def _():
                    copy1(wave, row, side).start()

    for side in range(2):

        @pl.when(my_side == side)
        def _():
            mid[me, :, piece(side)] = own[my_group, :, piece(side)]

    gram[...] = jnp.zeros_like(gram)

    for side in range(2):

        @pl.when(my_side == side)
        def _():
            @pl.loop(0, TEAM)
            def _(s):
                @pl.when(s != me)
                def _():
                    arrive1(s, side).wait_recv()

            @pl.loop(0, TEAM)
            def _(k):
                e = lax.rem(me + k, TEAM)
                stage[e, :, piece(side)] = mid[holder[e], :, piece(side)]

                @pl.when(e == me)
                def _():
                    slots[0, my_group, :, piece(side)] = stage[e, :, piece(side)]

                @pl.when(e != me)
                def _():
                    copy2(e, side).start()

    def part(first_group, count):
        return pl.ds(first_group, count)

    half = GROUPS // 2
    lower, upper = part(0, half), part(half, half)

    def copy_up(src, src_part, t, dst_part, sem):
        return pltpu.make_async_remote_copy(
            src_ref=slots.at[src, src_part],
            dst_ref=slots.at[t, dst_part],
            send_sem=send_up.at[sem],
            recv_sem=recv_up.at[sem],
            device_id=(up, me),
            device_id_type=MESH,
        )

    def copy_down(src, src_part, t, dst_part, sem):
        return pltpu.make_async_remote_copy(
            src_ref=slots.at[src, src_part],
            dst_ref=slots.at[t, dst_part],
            send_sem=send_down.at[sem],
            recv_sem=recv_down.at[sem],
            device_id=(down, me),
            device_id_type=MESH,
        )

    def copy_sib(t):
        return pltpu.make_async_remote_copy(
            src_ref=slots.at[t, part(0, GROUPS)],
            dst_ref=slots.at[t, part(GROUPS, GROUPS)],
            send_sem=send_sib.at[t],
            recv_sem=recv_sib.at[t],
            device_id=(sib, me),
            device_id_type=MESH,
        )

    def down_piece(src, t, p):
        rows = part(half + 2 * p, 2)
        return copy_down(src, rows, t, rows, STEPS - 2 + 2 * (t - (STEPS - 2)) + p)

    for wave in range(2):

        @pl.loop(0, 4)
        def _(row):
            for side in range(2):

                @pl.when(relay_of(wave, row, side) != me)
                def _():
                    arrive2(wave, row, side).wait_recv()

        sent = part(4 * wave, 4)
        copy_up(0, sent, wave + 1, lower, wave + 1).start()
        copy_down(0, sent, wave + 1, upper, wave + 1).start()

    def turn(t):
        turned[...] = slots[t].reshape(2 * ROWS, F).T

    def columns(t, start, size):
        return slots[t, :, :, start : start + size].reshape(2 * ROWS, size)

    def meet(t):
        copy_sib(t).wait_recv()
        turn(t)

    copy_sib(0).start()

    @pl.loop(0, STEPS - 1)
    def _(k):
        t = k + 1

        @pl.when(t == STEPS - 2)
        def _():
            for p in range(2):
                down_piece(4, 6, p).wait_recv()
                down_piece(6, 7, p).start()
            copy_up(4, lower, 6, lower, 6).wait_recv()
            copy_sib(t).start()

        @pl.when(t < STEPS - 2)
        def _():
            copy_up(t, lower, t, lower, t).wait_recv()
            copy_up(t, lower, t + 2, lower, t + 2).start()
            copy_down(t, upper, t, upper, t).wait_recv()

            @pl.when(t < STEPS - 4)
            def _():
                copy_down(t, upper, t + 2, upper, t + 2).start()

            @pl.when(t == STEPS - 4)
            def _():
                for p in range(2):
                    down_piece(4, 6, p).start()

            copy_sib(t).start()

        meet(k)
        for start, size in PANELS:
            end = start + size
            gram[0:end, start:end] += jnp.dot(
                turned[0:end, :], columns(k, start, size), preferred_element_type=jnp.float32
            )

    last = STEPS - 1
    copy_up(5, lower, last, lower, last).wait_recv()
    for p in range(2):
        down_piece(6, last, p).wait_recv()
    copy_sib(last).start()
    meet(last)
    squares = jnp.zeros((8, 128), jnp.float32)
    for start, size in PANELS:
        end = start + size
        panel = columns(last, start, size)
        for row, count in PANELS:
            if row > start:
                break
            rows = slice(row, row + count)
            g = gram[rows, start:end] + jnp.dot(
                turned[rows, :], panel, preferred_element_type=jnp.float32
            )
            amat[rows, start:end] = g.astype(jnp.bfloat16)
            folded = jnp.sum((g * g).reshape(count // 8, 8, size), axis=0)
            for lane in range(0, size, 128):
                lanes = folded[:, lane : lane + 128]
                squares = squares + (lanes if row == start else 2.0 * lanes)
        if start:
            amat[start:end, 0:start] = amat[0:start, start:end].T
    norm = jnp.sqrt(jnp.sum(squares, keepdims=True)) + gram_eps
    inverse = 1.0 / norm
    factor = 1.0 / jnp.sqrt(norm)

    def product(src, finish):
        for start, size in PANELS:
            cols = slice(start, start + size)
            finish(
                cols,
                inverse
                * jnp.dot(src[...], amat[:, cols], preferred_element_type=jnp.float32),
            )

    def poly(src, spare, finish):
        def linear(cols, u):
            base[:, cols] = coef_a * base[:, cols] + coef_b * u
            spare[:, cols] = u.astype(jnp.bfloat16)

        def quadratic(cols, u):
            finish(cols, base[:, cols] + coef_c * u)

        product(src, linear)
        product(spare, quadratic)

    def keep(dst):
        def finish(cols, value):
            base[:, cols] = value
            dst[:, cols] = value.astype(jnp.bfloat16)

        return finish

    def first(cols, value):
        y = (factor * value).astype(jnp.bfloat16)
        left[:, cols] = y
        base[:, cols] = y.astype(jnp.float32)
        total[:, cols] = coef_a * y.astype(jnp.float32)

    def second(cols, value):
        keep(right)(cols, value)
        total[:, cols] += coef_b * value

    def third(cols, value):
        result = total[:, cols] + coef_c * value
        out_ref[:, cols] = (math.sqrt(max(D, F)) * result).astype(jnp.bfloat16)

    left[...] = slots[0, 0:GROUPS].reshape(ROWS, F)
    base[...] = left[...].astype(jnp.float32)
    poly(left, right, first)
    poly(left, right, keep(left))
    product(left, keep(right))
    poly(right, left, second)
    poly(right, left, keep(right))
    product(right, keep(left))
    poly(left, right, third)

    for wave in range(2):

        @pl.loop(0, 4)
        def _(row):
            for side in range(2):

                @pl.when(relay_of(wave, row, side) != me)
                def _():
                    copy1(wave, row, side).wait_send()

    for side in range(2):

        @pl.when(my_side == side)
        def _():
            @pl.loop(0, TEAM)
            def _(e):
                @pl.when(e != me)
                def _():
                    copy2(e, side).wait_send()

    @pl.loop(0, STEPS)
    def _(t):
        copy_sib(t).wait_send()

        @pl.when(t > 0)
        def _():
            copy_up(t, lower, t, lower, t).wait_send()

            @pl.when(t < STEPS - 2)
            def _():
                copy_down(t, upper, t, upper, t).wait_send()

    for p in range(2):
        down_piece(4, 6, p).wait_send()
        down_piece(6, 7, p).wait_send()


def body(grad, expert_ids):
    dma = pltpu.SemaphoreType.DMA
    bf16, f32 = jnp.bfloat16, jnp.float32
    out = pl.pallas_call(
        kernel,
        out_shape=jax.ShapeDtypeStruct((ROWS, F), bf16),
        in_specs=[pl.BlockSpec(memory_space=pl.ANY)] * 2,
        out_specs=pl.BlockSpec(memory_space=pltpu.VMEM),
        scratch_shapes=[
            pltpu.VMEM((ROWS, F), f32),
            pltpu.SMEM((TEAM,), jnp.int32),
            pltpu.SMEM((TEAM,), jnp.int32),
            pltpu.VMEM((GROUPS, GROUP, F), bf16),
            pltpu.VMEM((TEAM, GROUP, F), bf16),
            pltpu.VMEM((TEAM, GROUP, F), bf16),
            pltpu.VMEM((STEPS, 2 * GROUPS, GROUP, F), bf16),
            pltpu.VMEM((F, 2 * ROWS), bf16),
            pltpu.VMEM((F, F), f32),
            pltpu.VMEM((F, F), bf16),
            pltpu.VMEM((ROWS, F), f32),
            pltpu.VMEM((ROWS, F), f32),
            pltpu.VMEM((ROWS, F), bf16),
            pltpu.VMEM((ROWS, F), bf16),
            dma,
            dma,
            dma((2 * GROUPS,)),
            dma((TEAM,)),
            dma((TEAM,)),
            dma((2 * GROUPS,)),
            dma((STEPS,)),
            dma((STEPS,)),
            dma((STEPS + 2,)),
            dma((STEPS + 2,)),
            dma((STEPS,)),
            dma((STEPS,)),
        ],
        compiler_params=pltpu.CompilerParams(
            collective_id=0,
            has_side_effects=True,
            vmem_limit_bytes=55800000,
        ),
        cost_estimate=pl.CostEstimate(
            flops=2 * F * F * (D + 12 * ROWS), bytes_accessed=6 * ROWS * F, transcendentals=0
        ),
    )(grad.reshape(ROWS, F), expert_ids)
    return out.reshape(1, ROWS, F)


def solution(mesh):
    return jax.shard_map(
        body,
        mesh=mesh,
        in_specs=(P("expert", "dp", None), P()),
        out_specs=P("expert", "dp", None),
        check_vma=False,
    )
```

```python
import math

import jax
import jax.numpy as jnp
from jax import lax
from jax.experimental import pallas as pl
from jax.experimental.pallas import tpu as pltpu
from jax.sharding import PartitionSpec as P

D = 2048
F = 1408
ROWS = 128
GROUP = 16
GROUPS = 8
TEAM = 16
RING = 8
STEPS = 8

coef_a = 3.4445
coef_b = -4.775
coef_c = 2.0315
gram_eps = 1e-07

MESH = pl.DeviceIdType.MESH
SPLIT = [(0, 640), (640, 768)]
WIDE = [(0, F)]
PANELS = [(i, min(256, F - i)) for i in range(0, F, 256)]


def kernel(
    grad_ref,
    ids_ref,
    out_ref,
    raw,
    ids,
    holder,
    own,
    mid,
    stage,
    slots,
    turned,
    gram,
    amat,
    base,
    total,
    left,
    right,
    load_raw,
    load_ids,
    send1,
    recv1,
    send2,
    recv2,
    send_up,
    recv_up,
    send_down,
    recv_down,
    send_sib,
    recv_sib,
):
    dp = lax.axis_index("dp")
    me = lax.axis_index("expert")
    core = lax.rem(dp, 2)
    z = dp // 2
    sib = dp + 1 - 2 * core
    up = lax.rem(z + 1, RING) * 2 + core
    down = lax.rem(z + RING - 1, RING) * 2 + core

    fetch_raw = pltpu.make_async_copy(grad_ref, raw, load_raw)
    fetch_ids = pltpu.make_async_copy(ids_ref, ids, load_ids)
    fetch_raw.start()
    fetch_ids.start()
    barrier = pltpu.get_barrier_semaphore()

    @pl.loop(1, TEAM)
    def _(k):
        pl.semaphore_signal(
            barrier, inc=1, device_id=(dp, lax.rem(me + k, TEAM)), device_id_type=MESH
        )

    for other in (sib, up, down):
        pl.semaphore_signal(barrier, inc=1, device_id=(other, me), device_id_type=MESH)
    fetch_raw.wait()
    own[...] = raw[...].reshape(GROUPS, GROUP, F).astype(jnp.bfloat16)
    fetch_ids.wait()

    @pl.loop(0, TEAM)
    def _(e):
        slot = jnp.int32(0)
        for j in range(TEAM):
            slot = jnp.where(ids[j] == e, j, slot)
        holder[e] = slot

    pl.semaphore_wait(barrier, TEAM + 2)

    def relay_of(wave, row, side):
        return 4 * row + 2 * side + lax.rem(row + wave + core, 2)

    my_x, my_y = lax.rem(me, 4), me // 4
    my_group = 4 * lax.rem(my_x + my_y + core, 2) + my_y
    my_side = my_x // 2

    def piece(side):
        return pl.ds(*SPLIT[side])

    def copy1(wave, row, side):
        g = 4 * wave + row
        return pltpu.make_async_remote_copy(
            src_ref=own.at[g, :, piece(side)],
            dst_ref=mid.at[me, :, piece(side)],
            send_sem=send1.at[2 * g + side],
            recv_sem=recv1.at[me],
            device_id=(dp, relay_of(wave, row, side)),
            device_id_type=MESH,
        )

    def arrive1(s, side):
        return pltpu.make_async_remote_copy(
            src_ref=own.at[0, :, piece(side)],
            dst_ref=mid.at[s, :, piece(side)],
            send_sem=send1.at[0],
            recv_sem=recv1.at[s],
            device_id=(dp, s),
            device_id_type=MESH,
        )

    def copy2(e, side):
        return pltpu.make_async_remote_copy(
            src_ref=stage.at[e, :, piece(side)],
            dst_ref=slots.at[0, my_group, :, piece(side)],
            send_sem=send2.at[e],
            recv_sem=recv2.at[2 * my_group + side],
            device_id=(dp, e),
            device_id_type=MESH,
        )

    def arrive2(wave, row, side):
        g = 4 * wave + row
        return pltpu.make_async_remote_copy(
            src_ref=stage.at[0, :, piece(side)],
            dst_ref=slots.at[0, g, :, piece(side)],
            send_sem=send2.at[0],
            recv_sem=recv2.at[2 * g + side],
            device_id=(dp, relay_of(wave, row, side)),
            device_id_type=MESH,
        )

    for wave in range(2):

        @pl.loop(0, 4)
        def _(k):
            row = lax.rem(k + me, 4)
            for side in range(2):

                @pl.when(relay_of(wave, row, side) != me)
                def _():
                    copy1(wave, row, side).start()

    for side in range(2):

        @pl.when(my_side == side)
        def _():
            mid[me, :, piece(side)] = own[my_group, :, piece(side)]

    gram[...] = jnp.zeros_like(gram)

    for side in range(2):

        @pl.when(my_side == side)
        def _():
            @pl.loop(0, TEAM)
            def _(s):
                @pl.when(s != me)
                def _():
                    arrive1(s, side).wait_recv()

            @pl.loop(0, TEAM)
            def _(k):
                e = lax.rem(me + k, TEAM)
                stage[e, :, piece(side)] = mid[holder[e], :, piece(side)]

                @pl.when(e == me)
                def _():
                    slots[0, my_group, :, piece(side)] = stage[e, :, piece(side)]

                @pl.when(e != me)
                def _():
                    copy2(e, side).start()

    def part(first_group, count):
        return pl.ds(first_group, count)

    half = GROUPS // 2
    lower, upper = part(0, half), part(half, half)

    def copy_up(src, src_part, t, dst_part, sem):
        return pltpu.make_async_remote_copy(
            src_ref=slots.at[src, src_part],
            dst_ref=slots.at[t, dst_part],
            send_sem=send_up.at[sem],
            recv_sem=recv_up.at[sem],
            device_id=(up, me),
            device_id_type=MESH,
        )

    def copy_down(src, src_part, t, dst_part, sem):
        return pltpu.make_async_remote_copy(
            src_ref=slots.at[src, src_part],
            dst_ref=slots.at[t, dst_part],
            send_sem=send_down.at[sem],
            recv_sem=recv_down.at[sem],
            device_id=(down, me),
            device_id_type=MESH,
        )

    def copy_sib(t):
        return pltpu.make_async_remote_copy(
            src_ref=slots.at[t, part(0, GROUPS)],
            dst_ref=slots.at[t, part(GROUPS, GROUPS)],
            send_sem=send_sib.at[t],
            recv_sem=recv_sib.at[t],
            device_id=(sib, me),
            device_id_type=MESH,
        )

    def down_piece(src, t, p):
        rows = part(half + 2 * p, 2)
        return copy_down(src, rows, t, rows, STEPS - 2 + 2 * (t - (STEPS - 2)) + p)

    for wave in range(2):

        @pl.loop(0, 4)
        def _(row):
            for side in range(2):

                @pl.when(relay_of(wave, row, side) != me)
                def _():
                    arrive2(wave, row, side).wait_recv()

        sent = part(4 * wave, 4)
        copy_up(0, sent, wave + 1, lower, wave + 1).start()
        copy_down(0, sent, wave + 1, upper, wave + 1).start()

    def turn(t):
        turned[...] = slots[t].reshape(2 * ROWS, F).T

    def columns(t, start, size):
        return slots[t, :, :, start : start + size].reshape(2 * ROWS, size)

    def meet(t):
        copy_sib(t).wait_recv()
        turn(t)

    copy_sib(0).start()

    @pl.loop(0, STEPS - 1)
    def _(k):
        t = k + 1

        @pl.when(t == STEPS - 2)
        def _():
            for p in range(2):
                down_piece(4, 6, p).wait_recv()
                down_piece(6, 7, p).start()
            copy_up(4, lower, 6, lower, 6).wait_recv()
            copy_sib(t).start()

        @pl.when(t < STEPS - 2)
        def _():
            copy_up(t, lower, t, lower, t).wait_recv()
            copy_up(t, lower, t + 2, lower, t + 2).start()
            copy_down(t, upper, t, upper, t).wait_recv()

            @pl.when(t < STEPS - 4)
            def _():
                copy_down(t, upper, t + 2, upper, t + 2).start()

            @pl.when(t == STEPS - 4)
            def _():
                for p in range(2):
                    down_piece(4, 6, p).start()

            copy_sib(t).start()

        meet(k)
        for start, size in PANELS:
            end = start + size
            gram[0:end, start:end] += jnp.dot(
                turned[0:end, :], columns(k, start, size), preferred_element_type=jnp.float32
            )

    last = STEPS - 1
    copy_up(5, lower, last, lower, last).wait_recv()
    for p in range(2):
        down_piece(6, last, p).wait_recv()
    copy_sib(last).start()
    meet(last)
    squares = jnp.zeros((8, 128), jnp.float32)
    for start, size in PANELS:
        end = start + size
        panel = columns(last, start, size)
        for row, count in PANELS:
            if row > start:
                break
            rows = slice(row, row + count)
            g = gram[rows, start:end] + jnp.dot(
                turned[rows, :], panel, preferred_element_type=jnp.float32
            )
            amat[rows, start:end] = g.astype(jnp.bfloat16)
            folded = jnp.sum((g * g).reshape(count // 8, 8, size), axis=0)
            for lane in range(0, size, 128):
                lanes = folded[:, lane : lane + 128]
                squares = squares + (lanes if row == start else 2.0 * lanes)
        if start:
            amat[start:end, 0:start] = amat[0:start, start:end].T
    norm = jnp.sqrt(jnp.sum(squares, keepdims=True)) + gram_eps
    inverse = 1.0 / norm
    factor = 1.0 / jnp.sqrt(norm)

    def product(src, finish):
        for start, size in WIDE:
            cols = slice(start, start + size)
            finish(
                cols,
                inverse
                * jnp.dot(src[...], amat[:, cols], preferred_element_type=jnp.float32),
            )

    def poly(src, spare, finish):
        def linear(cols, u):
            base[:, cols] = coef_a * base[:, cols] + coef_b * u
            spare[:, cols] = u.astype(jnp.bfloat16)

        def quadratic(cols, u):
            finish(cols, base[:, cols] + coef_c * u)

        product(src, linear)
        product(spare, quadratic)

    def keep(dst):
        def finish(cols, value):
            base[:, cols] = value
            dst[:, cols] = value.astype(jnp.bfloat16)

        return finish

    def first(cols, value):
        y = (factor * value).astype(jnp.bfloat16)
        left[:, cols] = y
        base[:, cols] = y.astype(jnp.float32)
        total[:, cols] = coef_a * y.astype(jnp.float32)

    def second(cols, value):
        keep(right)(cols, value)
        total[:, cols] += coef_b * value

    def third(cols, value):
        result = total[:, cols] + coef_c * value
        out_ref[:, cols] = (math.sqrt(max(D, F)) * result).astype(jnp.bfloat16)

    left[...] = slots[0, 0:GROUPS].reshape(ROWS, F)
    base[...] = left[...].astype(jnp.float32)
    poly(left, right, first)
    poly(left, right, keep(left))
    product(left, keep(right))
    poly(right, left, second)
    poly(right, left, keep(right))
    product(right, keep(left))
    poly(left, right, third)

    for wave in range(2):

        @pl.loop(0, 4)
        def _(row):
            for side in range(2):

                @pl.when(relay_of(wave, row, side) != me)
                def _():
                    copy1(wave, row, side).wait_send()

    for side in range(2):

        @pl.when(my_side == side)
        def _():
            @pl.loop(0, TEAM)
            def _(e):
                @pl.when(e != me)
                def _():
                    copy2(e, side).wait_send()

    @pl.loop(0, STEPS)
    def _(t):
        copy_sib(t).wait_send()

        @pl.when(t > 0)
        def _():
            copy_up(t, lower, t, lower, t).wait_send()

            @pl.when(t < STEPS - 2)
            def _():
                copy_down(t, upper, t, upper, t).wait_send()

    for p in range(2):
        down_piece(4, 6, p).wait_send()
        down_piece(6, 7, p).wait_send()


def body(grad, expert_ids):
    dma = pltpu.SemaphoreType.DMA
    bf16, f32 = jnp.bfloat16, jnp.float32
    out = pl.pallas_call(
        kernel,
        out_shape=jax.ShapeDtypeStruct((ROWS, F), bf16),
        in_specs=[pl.BlockSpec(memory_space=pl.ANY)] * 2,
        out_specs=pl.BlockSpec(memory_space=pltpu.VMEM),
        scratch_shapes=[
            pltpu.VMEM((ROWS, F), f32),
            pltpu.SMEM((TEAM,), jnp.int32),
            pltpu.SMEM((TEAM,), jnp.int32),
            pltpu.VMEM((GROUPS, GROUP, F), bf16),
            pltpu.VMEM((TEAM, GROUP, F), bf16),
            pltpu.VMEM((TEAM, GROUP, F), bf16),
            pltpu.VMEM((STEPS, 2 * GROUPS, GROUP, F), bf16),
            pltpu.VMEM((F, 2 * ROWS), bf16),
            pltpu.VMEM((F, F), f32),
            pltpu.VMEM((F, F), bf16),
            pltpu.VMEM((ROWS, F), f32),
            pltpu.VMEM((ROWS, F), f32),
            pltpu.VMEM((ROWS, F), bf16),
            pltpu.VMEM((ROWS, F), bf16),
            dma,
            dma,
            dma((2 * GROUPS,)),
            dma((TEAM,)),
            dma((TEAM,)),
            dma((2 * GROUPS,)),
            dma((STEPS,)),
            dma((STEPS,)),
            dma((STEPS + 2,)),
            dma((STEPS + 2,)),
            dma((STEPS,)),
            dma((STEPS,)),
        ],
        compiler_params=pltpu.CompilerParams(
            collective_id=0,
            has_side_effects=True,
            vmem_limit_bytes=55800000,
        ),
        cost_estimate=pl.CostEstimate(
            flops=2 * F * F * (D + 12 * ROWS), bytes_accessed=6 * ROWS * F, transcendentals=0
        ),
    )(grad.reshape(ROWS, F), expert_ids)
    return out.reshape(1, ROWS, F)


def solution(mesh):
    return jax.shard_map(
        body,
        mesh=mesh,
        in_specs=(P("expert", "dp", None), P()),
        out_specs=P("expert", "dp", None),
        check_vma=False,
    )
```

```python
import math

import jax
import jax.numpy as jnp
from jax import lax
from jax.experimental import pallas as pl
from jax.experimental.pallas import tpu as pltpu
from jax.sharding import PartitionSpec as P

D = 2048
F = 1408
ROWS = 128
GROUP = 16
GROUPS = 8
TEAM = 16
RING = 8
STEPS = 8

coef_a = 3.4445
coef_b = -4.775
coef_c = 2.0315
gram_eps = 1e-07

MESH = pl.DeviceIdType.MESH
SPLIT = [(0, 640), (640, 768)]
WIDE = [(0, F)]
PANELS = [(i, min(256, F - i)) for i in range(0, F, 256)]


def kernel(
    grad_ref,
    ids_ref,
    out_ref,
    raw,
    ids,
    holder,
    own,
    mid,
    stage,
    slots,
    turned,
    gram,
    amat,
    base,
    total,
    left,
    right,
    load_raw,
    load_ids,
    send1,
    recv1,
    send2,
    recv2,
    send_up,
    recv_up,
    send_down,
    recv_down,
    send_sib,
    recv_sib,
):
    dp = lax.axis_index("dp")
    me = lax.axis_index("expert")
    core = lax.rem(dp, 2)
    z = dp // 2
    sib = dp + 1 - 2 * core
    up = lax.rem(z + 1, RING) * 2 + core
    down = lax.rem(z + RING - 1, RING) * 2 + core

    fetch_raw = pltpu.make_async_copy(grad_ref, raw, load_raw)
    fetch_ids = pltpu.make_async_copy(ids_ref, ids, load_ids)
    fetch_raw.start()
    fetch_ids.start()
    barrier = pltpu.get_barrier_semaphore()

    @pl.loop(1, TEAM)
    def _(k):
        pl.semaphore_signal(
            barrier, inc=1, device_id=(dp, lax.rem(me + k, TEAM)), device_id_type=MESH
        )

    for other in (sib, up, down):
        pl.semaphore_signal(barrier, inc=1, device_id=(other, me), device_id_type=MESH)
    fetch_raw.wait()
    own[...] = raw[...].reshape(GROUPS, GROUP, F).astype(jnp.bfloat16)
    pl.semaphore_wait(barrier, TEAM + 2)

    def relay_of(wave, row, side):
        return 4 * row + 2 * side + lax.rem(row + wave + core, 2)

    my_x, my_y = lax.rem(me, 4), me // 4
    my_group = 4 * lax.rem(my_x + my_y + core, 2) + my_y
    my_side = my_x // 2

    def piece(side):
        return pl.ds(*SPLIT[side])

    def copy1(wave, row, side):
        g = 4 * wave + row
        return pltpu.make_async_remote_copy(
            src_ref=own.at[g, :, piece(side)],
            dst_ref=mid.at[me, :, piece(side)],
            send_sem=send1.at[2 * g + side],
            recv_sem=recv1.at[me],
            device_id=(dp, relay_of(wave, row, side)),
            device_id_type=MESH,
        )

    def arrive1(s, side):
        return pltpu.make_async_remote_copy(
            src_ref=own.at[0, :, piece(side)],
            dst_ref=mid.at[s, :, piece(side)],
            send_sem=send1.at[0],
            recv_sem=recv1.at[s],
            device_id=(dp, s),
            device_id_type=MESH,
        )

    def copy2(e, side):
        return pltpu.make_async_remote_copy(
            src_ref=stage.at[e, :, piece(side)],
            dst_ref=slots.at[0, my_group, :, piece(side)],
            send_sem=send2.at[e],
            recv_sem=recv2.at[2 * my_group + side],
            device_id=(dp, e),
            device_id_type=MESH,
        )

    def arrive2(wave, row, side):
        g = 4 * wave + row
        return pltpu.make_async_remote_copy(
            src_ref=stage.at[0, :, piece(side)],
            dst_ref=slots.at[0, g, :, piece(side)],
            send_sem=send2.at[0],
            recv_sem=recv2.at[2 * g + side],
            device_id=(dp, relay_of(wave, row, side)),
            device_id_type=MESH,
        )

    for wave in range(2):

        @pl.loop(0, 4)
        def _(k):
            row = lax.rem(k + me, 4)
            for side in range(2):

                @pl.when(relay_of(wave, row, side) != me)
                def _():
                    copy1(wave, row, side).start()

    for side in range(2):

        @pl.when(my_side == side)
        def _():
            mid[me, :, piece(side)] = own[my_group, :, piece(side)]

    fetch_ids.wait()

    @pl.loop(0, TEAM)
    def _(e):
        slot = jnp.int32(0)
        for j in range(TEAM):
            slot = jnp.where(ids[j] == e, j, slot)
        holder[e] = slot

    for side in range(2):

        @pl.when(my_side == side)
        def _():
            @pl.loop(0, TEAM)
            def _(s):
                @pl.when(s != me)
                def _():
                    arrive1(s, side).wait_recv()

            @pl.loop(0, TEAM)
            def _(k):
                e = lax.rem(me + k, TEAM)
                stage[e, :, piece(side)] = mid[holder[e], :, piece(side)]

                @pl.when(e == me)
                def _():
                    slots[0, my_group, :, piece(side)] = stage[e, :, piece(side)]

                @pl.when(e != me)
                def _():
                    copy2(e, side).start()

    def part(first_group, count):
        return pl.ds(first_group, count)

    half = GROUPS // 2
    lower, upper = part(0, half), part(half, half)

    def copy_up(src, src_part, t, dst_part, sem):
        return pltpu.make_async_remote_copy(
            src_ref=slots.at[src, src_part],
            dst_ref=slots.at[t, dst_part],
            send_sem=send_up.at[sem],
            recv_sem=recv_up.at[sem],
            device_id=(up, me),
            device_id_type=MESH,
        )

    def copy_down(src, src_part, t, dst_part, sem):
        return pltpu.make_async_remote_copy(
            src_ref=slots.at[src, src_part],
            dst_ref=slots.at[t, dst_part],
            send_sem=send_down.at[sem],
            recv_sem=recv_down.at[sem],
            device_id=(down, me),
            device_id_type=MESH,
        )

    def copy_sib(t):
        return pltpu.make_async_remote_copy(
            src_ref=slots.at[t, part(0, GROUPS)],
            dst_ref=slots.at[t, part(GROUPS, GROUPS)],
            send_sem=send_sib.at[t],
            recv_sem=recv_sib.at[t],
            device_id=(sib, me),
            device_id_type=MESH,
        )

    def down_piece(src, t, p):
        rows = part(half + 2 * p, 2)
        return copy_down(src, rows, t, rows, STEPS - 2 + 2 * (t - (STEPS - 2)) + p)

    gram[...] = jnp.zeros_like(gram)
    base[...] = jnp.zeros_like(base)

    for wave in range(2):

        @pl.loop(0, 4)
        def _(row):
            for side in range(2):

                @pl.when(relay_of(wave, row, side) != me)
                def _():
                    arrive2(wave, row, side).wait_recv()

        sent = part(4 * wave, 4)
        copy_up(0, sent, wave + 1, lower, wave + 1).start()
        copy_down(0, sent, wave + 1, upper, wave + 1).start()

    def turn(t):
        turned[...] = slots[t].reshape(2 * ROWS, F).T

    def columns(t, start, size):
        return slots[t, :, :, start : start + size].reshape(2 * ROWS, size)

    def meet(t):
        copy_sib(t).wait_recv()
        turn(t)

    copy_sib(0).start()
    left[...] = slots[0, 0:GROUPS].reshape(ROWS, F)

    def apply(t):
        inner = jnp.dot(left[...], turned[...], preferred_element_type=jnp.float32)
        base[...] += jnp.dot(
            inner.astype(jnp.bfloat16), columns(t, 0, F), preferred_element_type=jnp.float32
        )

    @pl.loop(0, STEPS - 1)
    def _(k):
        t = k + 1

        @pl.when(t == STEPS - 2)
        def _():
            for p in range(2):
                down_piece(4, 6, p).wait_recv()
                down_piece(6, 7, p).start()
            copy_up(4, lower, 6, lower, 6).wait_recv()
            copy_sib(t).start()

        @pl.when(t < STEPS - 2)
        def _():
            copy_up(t, lower, t, lower, t).wait_recv()
            copy_up(t, lower, t + 2, lower, t + 2).start()
            copy_down(t, upper, t, upper, t).wait_recv()

            @pl.when(t < STEPS - 4)
            def _():
                copy_down(t, upper, t + 2, upper, t + 2).start()

            @pl.when(t == STEPS - 4)
            def _():
                for p in range(2):
                    down_piece(4, 6, p).start()

            copy_sib(t).start()

        meet(k)
        for start, size in PANELS:
            end = start + size
            gram[0:end, start:end] += jnp.dot(
                turned[0:end, :], columns(k, start, size), preferred_element_type=jnp.float32
            )
        apply(k)

    last = STEPS - 1
    copy_up(5, lower, last, lower, last).wait_recv()
    for p in range(2):
        down_piece(6, last, p).wait_recv()
    copy_sib(last).start()
    meet(last)
    apply(last)
    squares = jnp.zeros((8, 128), jnp.float32)
    for start, size in PANELS:
        end = start + size
        panel = columns(last, start, size)
        for row, count in PANELS:
            if row > start:
                break
            rows = slice(row, row + count)
            g = gram[rows, start:end] + jnp.dot(
                turned[rows, :], panel, preferred_element_type=jnp.float32
            )
            amat[rows, start:end] = g.astype(jnp.bfloat16)
            folded = jnp.sum((g * g).reshape(count // 8, 8, size), axis=0)
            for lane in range(0, size, 128):
                lanes = folded[:, lane : lane + 128]
                squares = squares + (lanes if row == start else 2.0 * lanes)
        if start:
            amat[start:end, 0:start] = amat[0:start, start:end].T
    norm = jnp.sqrt(jnp.sum(squares, keepdims=True)) + gram_eps
    inverse = 1.0 / norm
    factor = 1.0 / jnp.sqrt(norm)

    def product(src, finish):
        for start, size in WIDE:
            cols = slice(start, start + size)
            finish(
                cols,
                inverse
                * jnp.dot(src[...], amat[:, cols], preferred_element_type=jnp.float32),
            )

    def linear(cols, x, u, spare):
        base[:, cols] = coef_a * x + coef_b * u
        spare[:, cols] = u.astype(jnp.bfloat16)

    def quadratic(spare, finish):
        product(spare, lambda cols, u: finish(cols, base[:, cols] + coef_c * u))

    def poly(src, spare, finish):
        product(src, lambda cols, u: linear(cols, base[:, cols], u, spare))
        quadratic(spare, finish)

    def keep(dst):
        def finish(cols, value):
            base[:, cols] = value
            dst[:, cols] = value.astype(jnp.bfloat16)

        return finish

    def first(cols, value):
        y = (factor * value).astype(jnp.bfloat16)
        left[:, cols] = y
        base[:, cols] = y.astype(jnp.float32)
        total[:, cols] = coef_a * y.astype(jnp.float32)

    def second(cols, value):
        keep(right)(cols, value)
        total[:, cols] += coef_b * value

    def third(cols, value):
        result = total[:, cols] + coef_c * value
        out_ref[:, cols] = (math.sqrt(max(D, F)) * result).astype(jnp.bfloat16)

    linear(slice(0, F), left[...].astype(jnp.float32), inverse * base[...], right)
    quadratic(right, first)
    poly(left, right, keep(left))
    product(left, keep(right))
    poly(right, left, second)
    poly(right, left, keep(right))
    product(right, keep(left))
    poly(left, right, third)

    for wave in range(2):

        @pl.loop(0, 4)
        def _(row):
            for side in range(2):

                @pl.when(relay_of(wave, row, side) != me)
                def _():
                    copy1(wave, row, side).wait_send()

    for side in range(2):

        @pl.when(my_side == side)
        def _():
            @pl.loop(0, TEAM)
            def _(e):
                @pl.when(e != me)
                def _():
                    copy2(e, side).wait_send()

    @pl.loop(0, STEPS)
    def _(t):
        copy_sib(t).wait_send()

        @pl.when(t > 0)
        def _():
            copy_up(t, lower, t, lower, t).wait_send()

            @pl.when(t < STEPS - 2)
            def _():
                copy_down(t, upper, t, upper, t).wait_send()

    for p in range(2):
        down_piece(4, 6, p).wait_send()
        down_piece(6, 7, p).wait_send()


def body(grad, expert_ids):
    dma = pltpu.SemaphoreType.DMA
    bf16, f32 = jnp.bfloat16, jnp.float32
    out = pl.pallas_call(
        kernel,
        out_shape=jax.ShapeDtypeStruct((ROWS, F), bf16),
        in_specs=[pl.BlockSpec(memory_space=pl.ANY)] * 2,
        out_specs=pl.BlockSpec(memory_space=pltpu.VMEM),
        scratch_shapes=[
            pltpu.VMEM((ROWS, F), f32),
            pltpu.SMEM((TEAM,), jnp.int32),
            pltpu.SMEM((TEAM,), jnp.int32),
            pltpu.VMEM((GROUPS, GROUP, F), bf16),
            pltpu.VMEM((TEAM, GROUP, F), bf16),
            pltpu.VMEM((TEAM, GROUP, F), bf16),
            pltpu.VMEM((STEPS, 2 * GROUPS, GROUP, F), bf16),
            pltpu.VMEM((F, 2 * ROWS), bf16),
            pltpu.VMEM((F, F), f32),
            pltpu.VMEM((F, F), bf16),
            pltpu.VMEM((ROWS, F), f32),
            pltpu.VMEM((ROWS, F), f32),
            pltpu.VMEM((ROWS, F), bf16),
            pltpu.VMEM((ROWS, F), bf16),
            dma,
            dma,
            dma((2 * GROUPS,)),
            dma((TEAM,)),
            dma((TEAM,)),
            dma((2 * GROUPS,)),
            dma((STEPS,)),
            dma((STEPS,)),
            dma((STEPS + 2,)),
            dma((STEPS + 2,)),
            dma((STEPS,)),
            dma((STEPS,)),
        ],
        compiler_params=pltpu.CompilerParams(
            collective_id=0,
            has_side_effects=True,
            vmem_limit_bytes=55800000,
        ),
        cost_estimate=pl.CostEstimate(
            flops=2 * F * F * (D + 12 * ROWS), bytes_accessed=6 * ROWS * F, transcendentals=0
        ),
    )(grad.reshape(ROWS, F), expert_ids)
    return out.reshape(1, ROWS, F)


def solution(mesh):
    return jax.shard_map(
        body,
        mesh=mesh,
        in_specs=(P("expert", "dp", None), P()),
        out_specs=P("expert", "dp", None),
        check_vma=False,
    )
```

```python
import math

import jax
import jax.numpy as jnp
from jax import lax
from jax.experimental import pallas as pl
from jax.experimental.pallas import tpu as pltpu
from jax.sharding import PartitionSpec as P

D = 2048
F = 1408
ROWS = 128
GROUP = 16
GROUPS = 8
TEAM = 16
RING = 8
STEPS = 8

coef_a = 3.4445
coef_b = -4.775
coef_c = 2.0315
gram_eps = 1e-07

MESH = pl.DeviceIdType.MESH
SPLIT = [(0, 640), (640, 768)]
WIDE = [(0, F)]
PANELS = [(i, min(256, F - i)) for i in range(0, F, 256)]


def kernel(
    grad_ref,
    ids_ref,
    out_ref,
    raw,
    ids,
    holder,
    own,
    mid,
    stage,
    slots,
    turned,
    gram,
    amat,
    base,
    total,
    left,
    right,
    load_raw,
    load_ids,
    send1,
    recv1,
    send2,
    recv2,
    send_up,
    recv_up,
    send_down,
    recv_down,
    send_sib,
    recv_sib,
):
    dp = lax.axis_index("dp")
    me = lax.axis_index("expert")
    core = lax.rem(dp, 2)
    z = dp // 2
    sib = dp + 1 - 2 * core
    up = lax.rem(z + 1, RING) * 2 + core
    down = lax.rem(z + RING - 1, RING) * 2 + core

    fetch_raw = pltpu.make_async_copy(grad_ref, raw, load_raw)
    fetch_ids = pltpu.make_async_copy(ids_ref, ids, load_ids)
    fetch_raw.start()
    fetch_ids.start()
    barrier = pltpu.get_barrier_semaphore()

    @pl.loop(1, TEAM)
    def _(k):
        pl.semaphore_signal(
            barrier, inc=1, device_id=(dp, lax.rem(me + k, TEAM)), device_id_type=MESH
        )

    for other in (sib, up, down):
        pl.semaphore_signal(barrier, inc=1, device_id=(other, me), device_id_type=MESH)
    fetch_raw.wait()
    own[...] = raw[...].reshape(GROUPS, GROUP, F).astype(jnp.bfloat16)
    pl.semaphore_wait(barrier, TEAM + 2)

    def relay_of(wave, row, side):
        return 4 * row + 2 * side + lax.rem(row + wave + core, 2)

    my_x, my_y = lax.rem(me, 4), me // 4
    my_group = 4 * lax.rem(my_x + my_y + core, 2) + my_y
    my_side = my_x // 2

    def piece(side):
        return pl.ds(*SPLIT[side])

    def copy1(wave, row, side):
        g = 4 * wave + row
        return pltpu.make_async_remote_copy(
            src_ref=own.at[g, :, piece(side)],
            dst_ref=mid.at[me, :, piece(side)],
            send_sem=send1.at[2 * g + side],
            recv_sem=recv1.at[me],
            device_id=(dp, relay_of(wave, row, side)),
            device_id_type=MESH,
        )

    def arrive1(s, side):
        return pltpu.make_async_remote_copy(
            src_ref=own.at[0, :, piece(side)],
            dst_ref=mid.at[s, :, piece(side)],
            send_sem=send1.at[0],
            recv_sem=recv1.at[s],
            device_id=(dp, s),
            device_id_type=MESH,
        )

    def copy2(e, side):
        return pltpu.make_async_remote_copy(
            src_ref=stage.at[e, :, piece(side)],
            dst_ref=slots.at[0, my_group, :, piece(side)],
            send_sem=send2.at[e],
            recv_sem=recv2.at[2 * my_group + side],
            device_id=(dp, e),
            device_id_type=MESH,
        )

    def arrive2(wave, row, side):
        g = 4 * wave + row
        return pltpu.make_async_remote_copy(
            src_ref=stage.at[0, :, piece(side)],
            dst_ref=slots.at[0, g, :, piece(side)],
            send_sem=send2.at[0],
            recv_sem=recv2.at[2 * g + side],
            device_id=(dp, relay_of(wave, row, side)),
            device_id_type=MESH,
        )

    for wave in range(2):

        @pl.loop(0, 4)
        def _(k):
            row = lax.rem(k + me, 4)
            for side in range(2):

                @pl.when(relay_of(wave, row, side) != me)
                def _():
                    copy1(wave, row, side).start()

    for side in range(2):

        @pl.when(my_side == side)
        def _():
            mid[me, :, piece(side)] = own[my_group, :, piece(side)]

    fetch_ids.wait()

    @pl.loop(0, TEAM)
    def _(e):
        slot = jnp.int32(0)
        for j in range(TEAM):
            slot = jnp.where(ids[j] == e, j, slot)
        holder[e] = slot

    for side in range(2):

        @pl.when(my_side == side)
        def _():
            @pl.loop(0, TEAM)
            def _(s):
                @pl.when(s != me)
                def _():
                    arrive1(s, side).wait_recv()

            @pl.loop(0, TEAM)
            def _(k):
                e = lax.rem(me + k, TEAM)
                stage[e, :, piece(side)] = mid[holder[e], :, piece(side)]

                @pl.when(e == me)
                def _():
                    slots[0, my_group, :, piece(side)] = stage[e, :, piece(side)]

                @pl.when(e != me)
                def _():
                    copy2(e, side).start()

    def part(first_group, count):
        return pl.ds(first_group, count)

    half = GROUPS // 2
    lower, upper = part(0, half), part(half, half)

    def copy_up(src, src_part, t, dst_part, sem):
        return pltpu.make_async_remote_copy(
            src_ref=slots.at[src, src_part],
            dst_ref=slots.at[t, dst_part],
            send_sem=send_up.at[sem],
            recv_sem=recv_up.at[sem],
            device_id=(up, me),
            device_id_type=MESH,
        )

    def copy_down(src, src_part, t, dst_part, sem):
        return pltpu.make_async_remote_copy(
            src_ref=slots.at[src, src_part],
            dst_ref=slots.at[t, dst_part],
            send_sem=send_down.at[sem],
            recv_sem=recv_down.at[sem],
            device_id=(down, me),
            device_id_type=MESH,
        )

    def copy_sib(t):
        return pltpu.make_async_remote_copy(
            src_ref=slots.at[t, part(0, GROUPS)],
            dst_ref=slots.at[t, part(GROUPS, GROUPS)],
            send_sem=send_sib.at[t],
            recv_sem=recv_sib.at[t],
            device_id=(sib, me),
            device_id_type=MESH,
        )

    def down_piece(src, t, p):
        rows = part(half + 2 * p, 2)
        return copy_down(src, rows, t, rows, STEPS - 2 + 2 * (t - (STEPS - 2)) + p)

    gram[...] = jnp.zeros_like(gram)
    base[...] = jnp.zeros_like(base)

    for wave in range(2):

        @pl.loop(0, 4)
        def _(row):
            for side in range(2):

                @pl.when(relay_of(wave, row, side) != me)
                def _():
                    arrive2(wave, row, side).wait_recv()

        sent = part(4 * wave, 4)
        copy_up(0, sent, wave + 1, lower, wave + 1).start()
        copy_down(0, sent, wave + 1, upper, wave + 1).start()

    def turn(t):
        turned[...] = slots[t].reshape(2 * ROWS, F).T

    def columns(t, start, size):
        return slots[t, :, :, start : start + size].reshape(2 * ROWS, size)

    def meet(t):
        copy_sib(t).wait_recv()
        turn(t)

    copy_sib(0).start()
    left[...] = slots[0, 0:GROUPS].reshape(ROWS, F)

    def apply(t):
        inner = jnp.dot(left[...], turned[...], preferred_element_type=jnp.float32)
        base[...] += jnp.dot(
            inner.astype(jnp.bfloat16), columns(t, 0, F), preferred_element_type=jnp.float32
        )

    @pl.loop(0, STEPS - 1)
    def _(k):
        t = k + 1

        @pl.when(t == STEPS - 2)
        def _():
            for p in range(2):
                down_piece(4, 6, p).wait_recv()
                down_piece(6, 7, p).start()
            copy_up(4, lower, 6, lower, 6).wait_recv()
            copy_sib(t).start()

        @pl.when(t < STEPS - 2)
        def _():
            copy_up(t, lower, t, lower, t).wait_recv()
            copy_up(t, lower, t + 2, lower, t + 2).start()
            copy_down(t, upper, t, upper, t).wait_recv()

            @pl.when(t < STEPS - 4)
            def _():
                copy_down(t, upper, t + 2, upper, t + 2).start()

            @pl.when(t == STEPS - 4)
            def _():
                for p in range(2):
                    down_piece(4, 6, p).start()

            copy_sib(t).start()

        meet(k)
        for start, size in PANELS:
            gram[:, start : start + size] += jnp.dot(
                turned[...], columns(k, start, size), preferred_element_type=jnp.float32
            )
        apply(k)

    last = STEPS - 1
    copy_up(5, lower, last, lower, last).wait_recv()
    for p in range(2):
        down_piece(6, last, p).wait_recv()
    copy_sib(last).start()
    meet(last)
    apply(last)
    squares = jnp.zeros((8, 128), jnp.float32)
    for start, size in PANELS:
        end = start + size
        panel = columns(last, start, size)
        for row, count in PANELS:
            rows = slice(row, row + count)
            g = gram[rows, start:end] + jnp.dot(
                turned[rows, :], panel, preferred_element_type=jnp.float32
            )
            amat[rows, start:end] = g.astype(jnp.bfloat16)
            folded = jnp.sum((g * g).reshape(count // 8, 8, size), axis=0)
            for lane in range(0, size, 128):
                squares = squares + folded[:, lane : lane + 128]
    norm = jnp.sqrt(jnp.sum(squares, keepdims=True)) + gram_eps
    inverse = 1.0 / norm
    factor = 1.0 / jnp.sqrt(norm)

    def product(src, finish):
        for start, size in WIDE:
            cols = slice(start, start + size)
            finish(
                cols,
                inverse
                * jnp.dot(src[...], amat[:, cols], preferred_element_type=jnp.float32),
            )

    def linear(cols, x, u, spare):
        base[:, cols] = coef_a * x + coef_b * u
        spare[:, cols] = u.astype(jnp.bfloat16)

    def quadratic(spare, finish):
        product(spare, lambda cols, u: finish(cols, base[:, cols] + coef_c * u))

    def poly(src, spare, finish):
        product(src, lambda cols, u: linear(cols, base[:, cols], u, spare))
        quadratic(spare, finish)

    def keep(dst):
        def finish(cols, value):
            base[:, cols] = value
            dst[:, cols] = value.astype(jnp.bfloat16)

        return finish

    def first(cols, value):
        y = (factor * value).astype(jnp.bfloat16)
        left[:, cols] = y
        base[:, cols] = y.astype(jnp.float32)
        total[:, cols] = coef_a * y.astype(jnp.float32)

    def second(cols, value):
        keep(right)(cols, value)
        total[:, cols] += coef_b * value

    def third(cols, value):
        result = total[:, cols] + coef_c * value
        out_ref[:, cols] = (math.sqrt(max(D, F)) * result).astype(jnp.bfloat16)

    linear(slice(0, F), left[...].astype(jnp.float32), inverse * base[...], right)
    quadratic(right, first)
    poly(left, right, keep(left))
    product(left, keep(right))
    poly(right, left, second)
    poly(right, left, keep(right))
    product(right, keep(left))
    poly(left, right, third)

    for wave in range(2):

        @pl.loop(0, 4)
        def _(row):
            for side in range(2):

                @pl.when(relay_of(wave, row, side) != me)
                def _():
                    copy1(wave, row, side).wait_send()

    for side in range(2):

        @pl.when(my_side == side)
        def _():
            @pl.loop(0, TEAM)
            def _(e):
                @pl.when(e != me)
                def _():
                    copy2(e, side).wait_send()

    @pl.loop(0, STEPS)
    def _(t):
        copy_sib(t).wait_send()

        @pl.when(t > 0)
        def _():
            copy_up(t, lower, t, lower, t).wait_send()

            @pl.when(t < STEPS - 2)
            def _():
                copy_down(t, upper, t, upper, t).wait_send()

    for p in range(2):
        down_piece(4, 6, p).wait_send()
        down_piece(6, 7, p).wait_send()


def body(grad, expert_ids):
    dma = pltpu.SemaphoreType.DMA
    bf16, f32 = jnp.bfloat16, jnp.float32
    out = pl.pallas_call(
        kernel,
        out_shape=jax.ShapeDtypeStruct((ROWS, F), bf16),
        in_specs=[pl.BlockSpec(memory_space=pl.ANY)] * 2,
        out_specs=pl.BlockSpec(memory_space=pltpu.VMEM),
        scratch_shapes=[
            pltpu.VMEM((ROWS, F), f32),
            pltpu.SMEM((TEAM,), jnp.int32),
            pltpu.SMEM((TEAM,), jnp.int32),
            pltpu.VMEM((GROUPS, GROUP, F), bf16),
            pltpu.VMEM((TEAM, GROUP, F), bf16),
            pltpu.VMEM((TEAM, GROUP, F), bf16),
            pltpu.VMEM((STEPS, 2 * GROUPS, GROUP, F), bf16),
            pltpu.VMEM((F, 2 * ROWS), bf16),
            pltpu.VMEM((F, F), f32),
            pltpu.VMEM((F, F), bf16),
            pltpu.VMEM((ROWS, F), f32),
            pltpu.VMEM((ROWS, F), f32),
            pltpu.VMEM((ROWS, F), bf16),
            pltpu.VMEM((ROWS, F), bf16),
            dma,
            dma,
            dma((2 * GROUPS,)),
            dma((TEAM,)),
            dma((TEAM,)),
            dma((2 * GROUPS,)),
            dma((STEPS,)),
            dma((STEPS,)),
            dma((STEPS + 2,)),
            dma((STEPS + 2,)),
            dma((STEPS,)),
            dma((STEPS,)),
        ],
        compiler_params=pltpu.CompilerParams(
            collective_id=0,
            has_side_effects=True,
            vmem_limit_bytes=55800000,
        ),
        cost_estimate=pl.CostEstimate(
            flops=2 * F * F * (D + 12 * ROWS), bytes_accessed=6 * ROWS * F, transcendentals=0
        ),
    )(grad.reshape(ROWS, F), expert_ids)
    return out.reshape(1, ROWS, F)


def solution(mesh):
    return jax.shard_map(
        body,
        mesh=mesh,
        in_specs=(P("expert", "dp", None), P()),
        out_specs=P("expert", "dp", None),
        check_vma=False,
    )
```

```python
import math

import jax
import jax.numpy as jnp
from jax import lax
from jax.experimental import pallas as pl
from jax.experimental.pallas import tpu as pltpu
from jax.sharding import PartitionSpec as P

D = 2048
F = 1408
ROWS = 128
GROUP = 16
GROUPS = 8
TEAM = 16
RING = 8
STEPS = 8

coef_a = 3.4445
coef_b = -4.775
coef_c = 2.0315
gram_eps = 1e-07

MESH = pl.DeviceIdType.MESH
SPLIT = [(0, 640), (640, 768)]
WIDE = [(0, F)]
PANELS = [(i, min(256, F - i)) for i in range(0, F, 256)]


def kernel(
    grad_ref,
    ids_ref,
    out_ref,
    raw,
    ids,
    holder,
    own,
    mid,
    stage,
    slots,
    turned,
    gram,
    amat,
    base,
    total,
    left,
    right,
    load_raw,
    load_ids,
    send1,
    recv1,
    send2,
    recv2,
    send_up,
    recv_up,
    send_down,
    recv_down,
    send_sib,
    recv_sib,
):
    dp = lax.axis_index("dp")
    me = lax.axis_index("expert")
    core = lax.rem(dp, 2)
    z = dp // 2
    sib = dp + 1 - 2 * core
    up = lax.rem(z + 1, RING) * 2 + core
    down = lax.rem(z + RING - 1, RING) * 2 + core

    fetch_raw = pltpu.make_async_copy(grad_ref, raw, load_raw)
    fetch_ids = pltpu.make_async_copy(ids_ref, ids, load_ids)
    fetch_raw.start()
    fetch_ids.start()
    barrier = pltpu.get_barrier_semaphore()

    @pl.loop(1, TEAM)
    def _(k):
        pl.semaphore_signal(
            barrier, inc=1, device_id=(dp, lax.rem(me + k, TEAM)), device_id_type=MESH
        )

    for other in (sib, up, down):
        pl.semaphore_signal(barrier, inc=1, device_id=(other, me), device_id_type=MESH)
    fetch_raw.wait()
    own[...] = raw[...].reshape(GROUPS, GROUP, F).astype(jnp.bfloat16)
    pl.semaphore_wait(barrier, TEAM + 2)

    def relay_of(wave, row, side):
        return 4 * row + 2 * side + lax.rem(row + wave + core, 2)

    my_x, my_y = lax.rem(me, 4), me // 4
    my_group = 4 * lax.rem(my_x + my_y + core, 2) + my_y
    my_side = my_x // 2

    def piece(side):
        return pl.ds(*SPLIT[side])

    def copy1(wave, row, side):
        g = 4 * wave + row
        return pltpu.make_async_remote_copy(
            src_ref=own.at[g, :, piece(side)],
            dst_ref=mid.at[me, :, piece(side)],
            send_sem=send1.at[2 * g + side],
            recv_sem=recv1.at[me],
            device_id=(dp, relay_of(wave, row, side)),
            device_id_type=MESH,
        )

    def arrive1(s, side):
        return pltpu.make_async_remote_copy(
            src_ref=own.at[0, :, piece(side)],
            dst_ref=mid.at[s, :, piece(side)],
            send_sem=send1.at[0],
            recv_sem=recv1.at[s],
            device_id=(dp, s),
            device_id_type=MESH,
        )

    def copy2(e, side):
        return pltpu.make_async_remote_copy(
            src_ref=stage.at[e, :, piece(side)],
            dst_ref=slots.at[0, my_group, :, piece(side)],
            send_sem=send2.at[e],
            recv_sem=recv2.at[2 * my_group + side],
            device_id=(dp, e),
            device_id_type=MESH,
        )

    def arrive2(wave, row, side):
        g = 4 * wave + row
        return pltpu.make_async_remote_copy(
            src_ref=stage.at[0, :, piece(side)],
            dst_ref=slots.at[0, g, :, piece(side)],
            send_sem=send2.at[0],
            recv_sem=recv2.at[2 * g + side],
            device_id=(dp, relay_of(wave, row, side)),
            device_id_type=MESH,
        )

    for wave in range(2):

        @pl.loop(0, 4)
        def _(k):
            row = lax.rem(k + me, 4)
            for side in range(2):

                @pl.when(relay_of(wave, row, side) != me)
                def _():
                    copy1(wave, row, side).start()

    for side in range(2):

        @pl.when(my_side == side)
        def _():
            mid[me, :, piece(side)] = own[my_group, :, piece(side)]

    fetch_ids.wait()
    values = [ids[j] for j in range(TEAM)]
    for e in range(TEAM):
        slot = jnp.int32(0)
        for j in range(TEAM):
            slot = jnp.where(values[j] == e, j, slot)
        holder[e] = slot

    for side in range(2):

        @pl.when(my_side == side)
        def _():
            @pl.loop(0, TEAM)
            def _(s):
                @pl.when(s != me)
                def _():
                    arrive1(s, side).wait_recv()

            for e in range(TEAM):
                stage[e, :, piece(side)] = mid[holder[e], :, piece(side)]

            @pl.loop(1, TEAM)
            def _(k):
                copy2(lax.rem(me + k, TEAM), side).start()

            slots[0, my_group, :, piece(side)] = stage[me, :, piece(side)]

    def part(first_group, count):
        return pl.ds(first_group, count)

    half = GROUPS // 2
    lower, upper = part(0, half), part(half, half)

    def copy_up(src, src_part, t, dst_part, sem):
        return pltpu.make_async_remote_copy(
            src_ref=slots.at[src, src_part],
            dst_ref=slots.at[t, dst_part],
            send_sem=send_up.at[sem],
            recv_sem=recv_up.at[sem],
            device_id=(up, me),
            device_id_type=MESH,
        )

    def copy_down(src, src_part, t, dst_part, sem):
        return pltpu.make_async_remote_copy(
            src_ref=slots.at[src, src_part],
            dst_ref=slots.at[t, dst_part],
            send_sem=send_down.at[sem],
            recv_sem=recv_down.at[sem],
            device_id=(down, me),
            device_id_type=MESH,
        )

    def copy_sib(t):
        return pltpu.make_async_remote_copy(
            src_ref=slots.at[t, part(0, GROUPS)],
            dst_ref=slots.at[t, part(GROUPS, GROUPS)],
            send_sem=send_sib.at[t],
            recv_sem=recv_sib.at[t],
            device_id=(sib, me),
            device_id_type=MESH,
        )

    def down_piece(src, t, p):
        rows = part(half + 2 * p, 2)
        return copy_down(src, rows, t, rows, STEPS - 2 + 2 * (t - (STEPS - 2)) + p)

    for wave in range(2):

        @pl.loop(0, 4)
        def _(row):
            for side in range(2):

                @pl.when(relay_of(wave, row, side) != me)
                def _():
                    arrive2(wave, row, side).wait_recv()

        if wave == 1:
            copy_sib(0).start()
            copy_up(0, lower, 1, lower, 1).wait_send()
            copy_down(0, lower, 1, upper, 1).wait_send()
        sent = part(4 * wave, 4)
        copy_up(0, sent, wave + 1, lower, wave + 1).start()
        copy_down(0, sent, wave + 1, upper, wave + 1).start()

    def turn(t, side):
        turned[:, side * ROWS : (side + 1) * ROWS] = (
            slots[t, side * GROUPS : (side + 1) * GROUPS].reshape(ROWS, F).T
        )

    def columns(t, start, size):
        return slots[t, :, :, start : start + size].reshape(2 * ROWS, size)

    def meet(t):
        turn(t, 0)
        copy_sib(t).wait_recv()
        turn(t, 1)

    gram[...] = jnp.zeros_like(gram)
    base[...] = jnp.zeros_like(base)
    left[...] = slots[0, 0:GROUPS].reshape(ROWS, F)

    def apply(t):
        inner = jnp.dot(left[...], turned[...], preferred_element_type=jnp.float32)
        base[...] += jnp.dot(
            inner.astype(jnp.bfloat16), columns(t, 0, F), preferred_element_type=jnp.float32
        )

    @pl.loop(0, STEPS - 1)
    def _(k):
        t = k + 1

        @pl.when(t == STEPS - 2)
        def _():
            for p in range(2):
                down_piece(4, 6, p).wait_recv()
                down_piece(6, 7, p).start()
            copy_up(4, lower, 6, lower, 6).wait_recv()
            copy_sib(t).start()

        @pl.when(t < STEPS - 2)
        def _():
            copy_up(t, lower, t, lower, t).wait_recv()
            copy_up(t, lower, t + 2, lower, t + 2).start()
            copy_down(t, upper, t, upper, t).wait_recv()

            @pl.when(t < STEPS - 4)
            def _():
                copy_down(t, upper, t + 2, upper, t + 2).start()

            @pl.when(t == STEPS - 4)
            def _():
                for p in range(2):
                    down_piece(4, 6, p).start()

            copy_sib(t).start()

        meet(k)
        for start, size in PANELS:
            end = start + size
            gram[0:end, start:end] += jnp.dot(
                turned[0:end, :], columns(k, start, size), preferred_element_type=jnp.float32
            )
        apply(k)

    for wave in range(2):

        @pl.loop(0, 4)
        def _(row):
            for side in range(2):

                @pl.when(relay_of(wave, row, side) != me)
                def _():
                    copy1(wave, row, side).wait_send()

    for side in range(2):

        @pl.when(my_side == side)
        def _():
            @pl.loop(1, TEAM)
            def _(k):
                copy2(lax.rem(me + k, TEAM), side).wait_send()

    @pl.loop(2, STEPS - 1)
    def _(t):
        copy_up(t, lower, t, lower, t).wait_send()

        @pl.when(t < STEPS - 2)
        def _():
            copy_down(t, upper, t, upper, t).wait_send()

    @pl.loop(0, STEPS - 1)
    def _(t):
        copy_sib(t).wait_send()

    for p in range(2):
        down_piece(4, 6, p).wait_send()

    last = STEPS - 1
    copy_up(5, lower, last, lower, last).wait_recv()
    for p in range(2):
        down_piece(6, last, p).wait_recv()
    copy_sib(last).start()
    meet(last)
    apply(last)
    squares = jnp.zeros((8, 128), jnp.float32)
    for start, size in PANELS:
        end = start + size
        panel = columns(last, start, size)
        for row, count in PANELS:
            if row > start:
                break
            rows = slice(row, row + count)
            g = gram[rows, start:end] + jnp.dot(
                turned[rows, :], panel, preferred_element_type=jnp.float32
            )
            amat[rows, start:end] = g.astype(jnp.bfloat16)
            folded = jnp.sum((g * g).reshape(count // 8, 8, size), axis=0)
            for lane in range(0, size, 128):
                lanes = folded[:, lane : lane + 128]
                squares = squares + (lanes if row == start else 2.0 * lanes)
        if start:
            amat[start:end, 0:start] = amat[0:start, start:end].T
    norm = jnp.sqrt(jnp.sum(squares, keepdims=True)) + gram_eps
    inverse = 1.0 / norm
    factor = 1.0 / jnp.sqrt(norm)

    def product(src, finish):
        for start, size in WIDE:
            cols = slice(start, start + size)
            finish(
                cols,
                inverse
                * jnp.dot(src[...], amat[:, cols], preferred_element_type=jnp.float32),
            )

    def linear(cols, x, u, spare):
        base[:, cols] = coef_a * x + coef_b * u
        spare[:, cols] = u.astype(jnp.bfloat16)

    def quadratic(spare, finish):
        product(spare, lambda cols, u: finish(cols, base[:, cols] + coef_c * u))

    def poly(src, spare, finish):
        product(src, lambda cols, u: linear(cols, base[:, cols], u, spare))
        quadratic(spare, finish)

    def keep(dst):
        def finish(cols, value):
            base[:, cols] = value
            dst[:, cols] = value.astype(jnp.bfloat16)

        return finish

    def first(cols, value):
        y = (factor * value).astype(jnp.bfloat16)
        left[:, cols] = y
        base[:, cols] = y.astype(jnp.float32)
        total[:, cols] = coef_a * y.astype(jnp.float32)

    def second(cols, value):
        keep(right)(cols, value)
        total[:, cols] += coef_b * value

    def third(cols, value):
        result = total[:, cols] + coef_c * value
        out_ref[:, cols] = (math.sqrt(max(D, F)) * result).astype(jnp.bfloat16)

    linear(slice(0, F), left[...].astype(jnp.float32), inverse * base[...], right)
    quadratic(right, first)
    poly(left, right, keep(left))
    product(left, keep(right))
    poly(right, left, second)
    poly(right, left, keep(right))
    product(right, keep(left))
    poly(left, right, third)

    down_piece(6, last, 0).wait_send()
    down_piece(6, last, 1).wait_send()
    copy_up(5, lower, last, lower, last).wait_send()
    copy_sib(last).wait_send()


def body(grad, expert_ids):
    dma = pltpu.SemaphoreType.DMA
    bf16, f32 = jnp.bfloat16, jnp.float32
    out = pl.pallas_call(
        kernel,
        out_shape=jax.ShapeDtypeStruct((ROWS, F), bf16),
        in_specs=[pl.BlockSpec(memory_space=pl.ANY)] * 2,
        out_specs=pl.BlockSpec(memory_space=pltpu.VMEM),
        scratch_shapes=[
            pltpu.VMEM((ROWS, F), f32),
            pltpu.SMEM((TEAM,), jnp.int32),
            pltpu.SMEM((TEAM,), jnp.int32),
            pltpu.VMEM((GROUPS, GROUP, F), bf16),
            pltpu.VMEM((TEAM, GROUP, F), bf16),
            pltpu.VMEM((TEAM, GROUP, F), bf16),
            pltpu.VMEM((STEPS, 2 * GROUPS, GROUP, F), bf16),
            pltpu.VMEM((F, 2 * ROWS), bf16),
            pltpu.VMEM((F, F), f32),
            pltpu.VMEM((F, F), bf16),
            pltpu.VMEM((ROWS, F), f32),
            pltpu.VMEM((ROWS, F), f32),
            pltpu.VMEM((ROWS, F), bf16),
            pltpu.VMEM((ROWS, F), bf16),
            dma,
            dma,
            dma((2 * GROUPS,)),
            dma((TEAM,)),
            dma((TEAM,)),
            dma((2 * GROUPS,)),
            dma((STEPS,)),
            dma((STEPS,)),
            dma((STEPS + 2,)),
            dma((STEPS + 2,)),
            dma((STEPS,)),
            dma((STEPS,)),
        ],
        compiler_params=pltpu.CompilerParams(
            collective_id=0,
            has_side_effects=True,
            vmem_limit_bytes=55800000,
        ),
        cost_estimate=pl.CostEstimate(
            flops=2 * F * F * (D + 12 * ROWS), bytes_accessed=6 * ROWS * F, transcendentals=0
        ),
    )(grad.reshape(ROWS, F), expert_ids)
    return out.reshape(1, ROWS, F)


def solution(mesh):
    return jax.shard_map(
        body,
        mesh=mesh,
        in_specs=(P("expert", "dp", None), P()),
        out_specs=P("expert", "dp", None),
        check_vma=False,
    )
```

```python
import math

import jax
import jax.numpy as jnp
from jax import lax
from jax.experimental import pallas as pl
from jax.experimental.pallas import tpu as pltpu
from jax.sharding import PartitionSpec as P

D = 2048
F = 1408
ROWS = 128
GROUP = 16
GROUPS = 8
TEAM = 16
RING = 8
STEPS = 8

coef_a = 3.4445
coef_b = -4.775
coef_c = 2.0315
gram_eps = 1e-07

MESH = pl.DeviceIdType.MESH
SPLIT = [(0, 640), (640, 768)]
WIDE = [(0, F)]
PANELS = [(i, min(256, F - i)) for i in range(0, F, 256)]


def kernel(
    grad_ref,
    ids_ref,
    out_ref,
    raw,
    ids,
    holder,
    own,
    mid,
    stage,
    slots,
    turned,
    gram,
    amat,
    base,
    total,
    left,
    right,
    load_raw,
    load_ids,
    send1,
    recv1,
    send2,
    recv2,
    send_up,
    recv_up,
    send_down,
    recv_down,
    send_sib,
    recv_sib,
):
    dp = lax.axis_index("dp")
    me = lax.axis_index("expert")
    core = lax.rem(dp, 2)
    z = dp // 2
    sib = dp + 1 - 2 * core
    up = lax.rem(z + 1, RING) * 2 + core
    down = lax.rem(z + RING - 1, RING) * 2 + core

    def fetch_raw(q):
        rows = pl.ds(32 * q, 32)
        return pltpu.make_async_copy(grad_ref.at[rows], raw.at[rows], load_raw.at[q])

    fetch_ids = pltpu.make_async_copy(ids_ref, ids, load_ids)
    for q in range(4):
        fetch_raw(q).start()
    fetch_ids.start()
    barrier = pltpu.get_barrier_semaphore()

    @pl.loop(1, TEAM)
    def _(k):
        pl.semaphore_signal(
            barrier, inc=1, device_id=(dp, lax.rem(me + k, TEAM)), device_id_type=MESH
        )

    for other in (sib, up, down):
        pl.semaphore_signal(barrier, inc=1, device_id=(other, me), device_id_type=MESH)
    fetch_ids.wait()
    values = [ids[j] for j in range(TEAM)]
    for e in range(TEAM):
        slot = jnp.int32(0)
        for j in range(TEAM):
            slot = jnp.where(values[j] == e, j, slot)
        holder[e] = slot

    pl.semaphore_wait(barrier, TEAM + 2)

    def swap(row):
        return row // 2 + 2 * lax.rem(row, 2)

    def relay_of(wave, row, side):
        y = swap(row)
        return 4 * y + 2 * side + lax.rem(y + wave + core, 2)

    my_x, my_y = lax.rem(me, 4), me // 4
    my_group = 4 * lax.rem(my_x + my_y + core, 2) + swap(my_y)
    my_side = my_x // 2

    def piece(side):
        return pl.ds(*SPLIT[side])

    def copy1(wave, row, side):
        g = 4 * wave + row
        return pltpu.make_async_remote_copy(
            src_ref=own.at[g, :, piece(side)],
            dst_ref=mid.at[me, :, piece(side)],
            send_sem=send1.at[2 * g + side],
            recv_sem=recv1.at[me],
            device_id=(dp, relay_of(wave, row, side)),
            device_id_type=MESH,
        )

    def arrive1(s, side):
        return pltpu.make_async_remote_copy(
            src_ref=own.at[0, :, piece(side)],
            dst_ref=mid.at[s, :, piece(side)],
            send_sem=send1.at[0],
            recv_sem=recv1.at[s],
            device_id=(dp, s),
            device_id_type=MESH,
        )

    def copy2(e, side):
        return pltpu.make_async_remote_copy(
            src_ref=stage.at[e, :, piece(side)],
            dst_ref=slots.at[0, my_group, :, piece(side)],
            send_sem=send2.at[e],
            recv_sem=recv2.at[2 * my_group + side],
            device_id=(dp, e),
            device_id_type=MESH,
        )

    def arrive2(wave, row, side):
        g = 4 * wave + row
        return pltpu.make_async_remote_copy(
            src_ref=stage.at[0, :, piece(side)],
            dst_ref=slots.at[0, g, :, piece(side)],
            send_sem=send2.at[0],
            recv_sem=recv2.at[2 * g + side],
            device_id=(dp, relay_of(wave, row, side)),
            device_id_type=MESH,
        )

    for q in range(4):
        fetch_raw(q).wait()
        own[2 * q : 2 * q + 2] = (
            raw[32 * q : 32 * q + 32].reshape(2, GROUP, F).astype(jnp.bfloat16)
        )
        wave = q // 2

        @pl.loop(0, 2)
        def _(k):
            row = 2 * (q % 2) + lax.rem(k + me, 2)
            for side in range(2):

                @pl.when(relay_of(wave, row, side) != me)
                def _():
                    copy1(wave, row, side).start()

    for side in range(2):

        @pl.when(my_side == side)
        def _():
            mid[me, :, piece(side)] = own[my_group, :, piece(side)]

    for side in range(2):

        @pl.when(my_side == side)
        def _():
            @pl.loop(0, TEAM)
            def _(s):
                @pl.when(s != me)
                def _():
                    arrive1(s, side).wait_recv()

            for e in range(TEAM):
                stage[e, :, piece(side)] = mid[holder[e], :, piece(side)]

            @pl.loop(1, TEAM)
            def _(k):
                copy2(lax.rem(me + k, TEAM), side).start()

            slots[0, my_group, :, piece(side)] = stage[me, :, piece(side)]

    def part(first_group, count):
        return pl.ds(first_group, count)

    def up_piece(src, first_group, t, p):
        return pltpu.make_async_remote_copy(
            src_ref=slots.at[src, part(first_group + 2 * p, 2)],
            dst_ref=slots.at[t, part(2 * p, 2)],
            send_sem=send_up.at[2 * t + p],
            recv_sem=recv_up.at[2 * t + p],
            device_id=(up, me),
            device_id_type=MESH,
        )

    def down_piece(src, first_group, t, p):
        return pltpu.make_async_remote_copy(
            src_ref=slots.at[src, part(first_group + 2 * p, 2)],
            dst_ref=slots.at[t, part(4 + 2 * p, 2)],
            send_sem=send_down.at[2 * t + p],
            recv_sem=recv_down.at[2 * t + p],
            device_id=(down, me),
            device_id_type=MESH,
        )

    def copy_sib(t):
        return pltpu.make_async_remote_copy(
            src_ref=slots.at[t, part(0, GROUPS)],
            dst_ref=slots.at[t, part(GROUPS, GROUPS)],
            send_sem=send_sib.at[t],
            recv_sem=recv_sib.at[t],
            device_id=(sib, me),
            device_id_type=MESH,
        )

    for wave in range(2):
        for p in range(2):

            @pl.loop(2 * p, 2 * p + 2)
            def _(row):
                for side in range(2):

                    @pl.when(relay_of(wave, row, side) != me)
                    def _():
                        arrive2(wave, row, side).wait_recv()

            up_piece(0, 4 * wave, wave + 1, p).start()
            down_piece(0, 4 * wave, wave + 1, p).start()
    copy_sib(0).start()

    def turn(t, side):
        turned[:, side * ROWS : (side + 1) * ROWS] = (
            slots[t, side * GROUPS : (side + 1) * GROUPS].reshape(ROWS, F).T
        )

    def columns(t, start, size):
        return slots[t, :, :, start : start + size].reshape(2 * ROWS, size)

    def meet(t):
        turn(t, 0)
        copy_sib(t).wait_recv()
        turn(t, 1)

    gram[...] = jnp.zeros_like(gram)
    base[...] = jnp.zeros_like(base)
    left[...] = slots[0, 0:GROUPS].reshape(ROWS, F)

    def apply(t):
        inner = jnp.dot(left[...], turned[...], preferred_element_type=jnp.float32)
        base[...] += jnp.dot(
            inner.astype(jnp.bfloat16), columns(t, 0, F), preferred_element_type=jnp.float32
        )

    @pl.loop(0, STEPS - 1)
    def _(k):
        t = k + 1

        @pl.when(t < STEPS - 1)
        def _():
            for p in range(2):
                up_piece(t, 0, t, p).wait_recv()

                @pl.when(t < STEPS - 2)
                def _():
                    up_piece(t, 0, t + 2, p).start()

                down_piece(t, 4, t, p).wait_recv()

                @pl.when(t < STEPS - 3)
                def _():
                    down_piece(t, 4, t + 2, p).start()

                @pl.when(t == STEPS - 2)
                def _():
                    down_piece(t, 4, t + 1, p).start()

            copy_sib(t).start()

        meet(k)
        for start, size in PANELS:
            end = start + size
            gram[0:end, start:end] += jnp.dot(
                turned[0:end, :], columns(k, start, size), preferred_element_type=jnp.float32
            )
        apply(k)

    for wave in range(2):

        @pl.loop(0, 4)
        def _(row):
            for side in range(2):

                @pl.when(relay_of(wave, row, side) != me)
                def _():
                    copy1(wave, row, side).wait_send()

    for side in range(2):

        @pl.when(my_side == side)
        def _():
            @pl.loop(1, TEAM)
            def _(k):
                copy2(lax.rem(me + k, TEAM), side).wait_send()

    @pl.loop(1, STEPS - 1)
    def _(t):
        for p in range(2):
            up_piece(t, 0, t, p).wait_send()
            down_piece(t, 4, t, p).wait_send()

    @pl.loop(0, STEPS - 1)
    def _(t):
        copy_sib(t).wait_send()

    last = STEPS - 1
    for p in range(2):
        up_piece(last, 0, last, p).wait_recv()
        down_piece(last, 4, last, p).wait_recv()
    copy_sib(last).start()
    meet(last)
    apply(last)
    squares = jnp.zeros((8, 128), jnp.float32)
    for start, size in PANELS:
        end = start + size
        panel = columns(last, start, size)
        for row, count in PANELS:
            if row > start:
                break
            rows = slice(row, row + count)
            g = gram[rows, start:end] + jnp.dot(
                turned[rows, :], panel, preferred_element_type=jnp.float32
            )
            amat[rows, start:end] = g.astype(jnp.bfloat16)
            folded = jnp.sum((g * g).reshape(count // 8, 8, size), axis=0)
            for lane in range(0, size, 128):
                lanes = folded[:, lane : lane + 128]
                squares = squares + (lanes if row == start else 2.0 * lanes)
        if start:
            amat[start:end, 0:start] = amat[0:start, start:end].T
    norm = jnp.sqrt(jnp.sum(squares, keepdims=True)) + gram_eps
    inverse = 1.0 / norm
    factor = 1.0 / jnp.sqrt(norm)

    def product(src, finish):
        for start, size in WIDE:
            cols = slice(start, start + size)
            finish(
                cols,
                inverse
                * jnp.dot(src[...], amat[:, cols], preferred_element_type=jnp.float32),
            )

    def linear(cols, x, u, spare):
        base[:, cols] = coef_a * x + coef_b * u
        spare[:, cols] = u.astype(jnp.bfloat16)

    def quadratic(spare, finish):
        product(spare, lambda cols, u: finish(cols, base[:, cols] + coef_c * u))

    def poly(src, spare, finish):
        product(src, lambda cols, u: linear(cols, base[:, cols], u, spare))
        quadratic(spare, finish)

    def keep(dst):
        def finish(cols, value):
            base[:, cols] = value
            dst[:, cols] = value.astype(jnp.bfloat16)

        return finish

    def first(cols, value):
        y = (factor * value).astype(jnp.bfloat16)
        left[:, cols] = y
        base[:, cols] = y.astype(jnp.float32)
        total[:, cols] = coef_a * y.astype(jnp.float32)

    def second(cols, value):
        keep(right)(cols, value)
        total[:, cols] += coef_b * value

    def third(cols, value):
        result = total[:, cols] + coef_c * value
        out_ref[:, cols] = (math.sqrt(max(D, F)) * result).astype(jnp.bfloat16)

    linear(slice(0, F), left[...].astype(jnp.float32), inverse * base[...], right)
    quadratic(right, first)
    poly(left, right, keep(left))
    product(left, keep(right))
    poly(right, left, second)
    poly(right, left, keep(right))
    product(right, keep(left))
    poly(left, right, third)

    for p in range(2):
        up_piece(last, 0, last, p).wait_send()
        down_piece(last, 4, last, p).wait_send()
    copy_sib(last).wait_send()


def body(grad, expert_ids):
    dma = pltpu.SemaphoreType.DMA
    bf16, f32 = jnp.bfloat16, jnp.float32
    out = pl.pallas_call(
        kernel,
        out_shape=jax.ShapeDtypeStruct((ROWS, F), bf16),
        in_specs=[pl.BlockSpec(memory_space=pl.ANY)] * 2,
        out_specs=pl.BlockSpec(memory_space=pltpu.VMEM),
        scratch_shapes=[
            pltpu.VMEM((ROWS, F), f32),
            pltpu.SMEM((TEAM,), jnp.int32),
            pltpu.SMEM((TEAM,), jnp.int32),
            pltpu.VMEM((GROUPS, GROUP, F), bf16),
            pltpu.VMEM((TEAM, GROUP, F), bf16),
            pltpu.VMEM((TEAM, GROUP, F), bf16),
            pltpu.VMEM((STEPS, 2 * GROUPS, GROUP, F), bf16),
            pltpu.VMEM((F, 2 * ROWS), bf16),
            pltpu.VMEM((F, F), f32),
            pltpu.VMEM((F, F), bf16),
            pltpu.VMEM((ROWS, F), f32),
            pltpu.VMEM((ROWS, F), f32),
            pltpu.VMEM((ROWS, F), bf16),
            pltpu.VMEM((ROWS, F), bf16),
            dma((4,)),
            dma,
            dma((2 * GROUPS,)),
            dma((TEAM,)),
            dma((TEAM,)),
            dma((2 * GROUPS,)),
            dma((2 * STEPS,)),
            dma((2 * STEPS,)),
            dma((2 * STEPS,)),
            dma((2 * STEPS,)),
            dma((STEPS,)),
            dma((STEPS,)),
        ],
        compiler_params=pltpu.CompilerParams(
            collective_id=0,
            has_side_effects=True,
            vmem_limit_bytes=55800000,
        ),
        cost_estimate=pl.CostEstimate(
            flops=2 * F * F * (D + 12 * ROWS), bytes_accessed=6 * ROWS * F, transcendentals=0
        ),
    )(grad.reshape(ROWS, F), expert_ids)
    return out.reshape(1, ROWS, F)


def solution(mesh):
    return jax.shard_map(
        body,
        mesh=mesh,
        in_specs=(P("expert", "dp", None), P()),
        out_specs=P("expert", "dp", None),
        check_vma=False,
    )
```

```python
import math

import jax
import jax.numpy as jnp
from jax import lax
from jax.experimental import pallas as pl
from jax.experimental.pallas import tpu as pltpu
from jax.sharding import PartitionSpec as P

D = 2048
F = 1408
ROWS = 128
GROUP = 16
GROUPS = 8
TEAM = 16
RING = 8
STEPS = 8

coef_a = 3.4445
coef_b = -4.775
coef_c = 2.0315
gram_eps = 1e-07

MESH = pl.DeviceIdType.MESH
SPLIT = [(0, 640), (640, 768)]
WIDE = [(0, F)]
PANELS = [(i, min(256, F - i)) for i in range(0, F, 256)]


def kernel(
    grad_ref,
    ids_ref,
    out_ref,
    raw,
    ids,
    holder,
    own,
    mid,
    stage,
    slots,
    turned,
    gram,
    amat,
    base,
    total,
    left,
    right,
    load_raw,
    load_ids,
    send1,
    recv1,
    send2,
    recv2,
    send_up,
    recv_up,
    send_down,
    recv_down,
    send_sib,
    recv_sib,
):
    dp = lax.axis_index("dp")
    me = lax.axis_index("expert")
    core = lax.rem(dp, 2)
    z = dp // 2
    sib = dp + 1 - 2 * core
    up = lax.rem(z + 1, RING) * 2 + core
    down = lax.rem(z + RING - 1, RING) * 2 + core

    def fetch_raw(q):
        rows = pl.ds(32 * q, 32)
        return pltpu.make_async_copy(grad_ref.at[rows], raw.at[rows], load_raw.at[q])

    fetch_ids = pltpu.make_async_copy(ids_ref, ids, load_ids)
    for q in range(4):
        fetch_raw(q).start()
    fetch_ids.start()
    barrier = pltpu.get_barrier_semaphore()

    @pl.loop(1, TEAM)
    def _(k):
        pl.semaphore_signal(
            barrier, inc=1, device_id=(dp, lax.rem(me + k, TEAM)), device_id_type=MESH
        )

    for other in (sib, up, down):
        pl.semaphore_signal(barrier, inc=1, device_id=(other, me), device_id_type=MESH)
    fetch_ids.wait()
    values = [ids[j] for j in range(TEAM)]
    for e in range(TEAM):
        slot = jnp.int32(0)
        for j in range(TEAM):
            slot = jnp.where(values[j] == e, j, slot)
        holder[e] = slot

    pl.semaphore_wait(barrier, TEAM + 2)

    def swap(row):
        return row // 2 + 2 * lax.rem(row, 2)

    def relay_of(wave, row, side):
        y = swap(row)
        return 4 * y + 2 * side + lax.rem(y + wave + core, 2)

    my_x, my_y = lax.rem(me, 4), me // 4
    my_group = 4 * lax.rem(my_x + my_y + core, 2) + swap(my_y)
    my_side = my_x // 2

    def piece(side):
        return pl.ds(*SPLIT[side])

    def copy1(wave, row, side):
        g = 4 * wave + row
        return pltpu.make_async_remote_copy(
            src_ref=own.at[g, :, piece(side)],
            dst_ref=mid.at[me, :, piece(side)],
            send_sem=send1.at[2 * g + side],
            recv_sem=recv1.at[me],
            device_id=(dp, relay_of(wave, row, side)),
            device_id_type=MESH,
        )

    def arrive1(s, side):
        return pltpu.make_async_remote_copy(
            src_ref=own.at[0, :, piece(side)],
            dst_ref=mid.at[s, :, piece(side)],
            send_sem=send1.at[0],
            recv_sem=recv1.at[s],
            device_id=(dp, s),
            device_id_type=MESH,
        )

    def copy2(e, side):
        return pltpu.make_async_remote_copy(
            src_ref=stage.at[e, :, piece(side)],
            dst_ref=slots.at[0, my_group, :, piece(side)],
            send_sem=send2.at[e],
            recv_sem=recv2.at[2 * my_group + side],
            device_id=(dp, e),
            device_id_type=MESH,
        )

    def arrive2(wave, row, side):
        g = 4 * wave + row
        return pltpu.make_async_remote_copy(
            src_ref=stage.at[0, :, piece(side)],
            dst_ref=slots.at[0, g, :, piece(side)],
            send_sem=send2.at[0],
            recv_sem=recv2.at[2 * g + side],
            device_id=(dp, relay_of(wave, row, side)),
            device_id_type=MESH,
        )

    for q in range(4):
        fetch_raw(q).wait()
        own[2 * q : 2 * q + 2] = (
            raw[32 * q : 32 * q + 32].reshape(2, GROUP, F).astype(jnp.bfloat16)
        )
        wave = q // 2

        @pl.loop(0, 2)
        def _(k):
            row = 2 * (q % 2) + lax.rem(k + me, 2)
            for side in range(2):

                @pl.when(relay_of(wave, row, side) != me)
                def _():
                    copy1(wave, row, side).start()

    for side in range(2):

        @pl.when(my_side == side)
        def _():
            mid[me, :, piece(side)] = own[my_group, :, piece(side)]

    for side in range(2):

        @pl.when(my_side == side)
        def _():
            @pl.loop(0, TEAM)
            def _(s):
                @pl.when(s != me)
                def _():
                    arrive1(s, side).wait_recv()

            for e in range(TEAM):
                stage[e, :, piece(side)] = mid[holder[e], :, piece(side)]

            @pl.loop(0, TEAM)
            def _(k):
                e = jnp.where(k == 0, 0, 1 + lax.rem(me + k, TEAM - 1))

                @pl.when(e != me)
                def _():
                    copy2(e, side).start()

            slots[0, my_group, :, piece(side)] = stage[me, :, piece(side)]

    def part(first_group, count):
        return pl.ds(first_group, count)

    def up_piece(src, first_group, t, p):
        return pltpu.make_async_remote_copy(
            src_ref=slots.at[src, part(first_group + 2 * p, 2)],
            dst_ref=slots.at[t, part(2 * p, 2)],
            send_sem=send_up.at[2 * t + p],
            recv_sem=recv_up.at[2 * t + p],
            device_id=(up, me),
            device_id_type=MESH,
        )

    def down_piece(src, first_group, t, p):
        return pltpu.make_async_remote_copy(
            src_ref=slots.at[src, part(first_group + 2 * p, 2)],
            dst_ref=slots.at[t, part(4 + 2 * p, 2)],
            send_sem=send_down.at[2 * t + p],
            recv_sem=recv_down.at[2 * t + p],
            device_id=(down, me),
            device_id_type=MESH,
        )

    def copy_sib(t):
        return pltpu.make_async_remote_copy(
            src_ref=slots.at[t, part(0, GROUPS)],
            dst_ref=slots.at[t, part(GROUPS, GROUPS)],
            send_sem=send_sib.at[t],
            recv_sem=recv_sib.at[t],
            device_id=(sib, me),
            device_id_type=MESH,
        )

    for wave in range(2):
        for p in range(2):

            @pl.loop(2 * p, 2 * p + 2)
            def _(row):
                for side in range(2):

                    @pl.when(relay_of(wave, row, side) != me)
                    def _():
                        arrive2(wave, row, side).wait_recv()

            up_piece(0, 4 * wave, wave + 1, p).start()
            down_piece(0, 4 * wave, wave + 1, p).start()
    copy_sib(0).start()

    def turn(t, side):
        turned[:, side * ROWS : (side + 1) * ROWS] = (
            slots[t, side * GROUPS : (side + 1) * GROUPS].reshape(ROWS, F).T
        )

    def columns(t, start, size):
        return slots[t, :, :, start : start + size].reshape(2 * ROWS, size)

    def meet(t):
        turn(t, 0)
        copy_sib(t).wait_recv()
        turn(t, 1)

    gram[...] = jnp.zeros_like(gram)
    base[...] = jnp.zeros_like(base)
    left[...] = slots[0, 0:GROUPS].reshape(ROWS, F)

    def apply(t):
        inner = jnp.dot(left[...], turned[...], preferred_element_type=jnp.float32)
        base[...] += jnp.dot(
            inner.astype(jnp.bfloat16), columns(t, 0, F), preferred_element_type=jnp.float32
        )

    @pl.loop(0, STEPS - 1)
    def _(k):
        t = k + 1

        @pl.when(t < STEPS - 1)
        def _():
            for p in range(2):
                up_piece(t, 0, t, p).wait_recv()

                @pl.when(t < STEPS - 2)
                def _():
                    up_piece(t, 0, t + 2, p).start()

                down_piece(t, 4, t, p).wait_recv()

                @pl.when(t < STEPS - 3)
                def _():
                    down_piece(t, 4, t + 2, p).start()

                @pl.when(t == STEPS - 2)
                def _():
                    down_piece(t, 4, t + 1, p).start()

            copy_sib(t).start()

        meet(k)
        for start, size in PANELS:
            end = start + size
            gram[0:end, start:end] += jnp.dot(
                turned[0:end, :], columns(k, start, size), preferred_element_type=jnp.float32
            )
        apply(k)

    for wave in range(2):

        @pl.loop(0, 4)
        def _(row):
            for side in range(2):

                @pl.when(relay_of(wave, row, side) != me)
                def _():
                    copy1(wave, row, side).wait_send()

    for side in range(2):

        @pl.when(my_side == side)
        def _():
            @pl.loop(1, TEAM)
            def _(k):
                copy2(lax.rem(me + k, TEAM), side).wait_send()

    @pl.loop(1, STEPS - 1)
    def _(t):
        for p in range(2):
            up_piece(t, 0, t, p).wait_send()
            down_piece(t, 4, t, p).wait_send()

    @pl.loop(0, STEPS - 1)
    def _(t):
        copy_sib(t).wait_send()

    last = STEPS - 1
    for p in range(2):
        up_piece(last, 0, last, p).wait_recv()
        down_piece(last, 4, last, p).wait_recv()
    copy_sib(last).start()
    meet(last)
    apply(last)
    squares = jnp.zeros((8, 128), jnp.float32)
    for start, size in PANELS:
        end = start + size
        panel = columns(last, start, size)
        for row, count in PANELS:
            if row > start:
                break
            rows = slice(row, row + count)
            g = gram[rows, start:end] + jnp.dot(
                turned[rows, :], panel, preferred_element_type=jnp.float32
            )
            amat[rows, start:end] = g.astype(jnp.bfloat16)
            folded = jnp.sum((g * g).reshape(count // 8, 8, size), axis=0)
            for lane in range(0, size, 128):
                lanes = folded[:, lane : lane + 128]
                squares = squares + (lanes if row == start else 2.0 * lanes)
        if start:
            amat[start:end, 0:start] = amat[0:start, start:end].T
    norm = jnp.sqrt(jnp.sum(squares, keepdims=True)) + gram_eps
    inverse = 1.0 / norm
    factor = 1.0 / jnp.sqrt(norm)

    def product(src, finish):
        for start, size in WIDE:
            cols = slice(start, start + size)
            finish(
                cols,
                inverse
                * jnp.dot(src[...], amat[:, cols], preferred_element_type=jnp.float32),
            )

    def linear(cols, x, u, spare):
        base[:, cols] = coef_a * x + coef_b * u
        spare[:, cols] = u.astype(jnp.bfloat16)

    def quadratic(spare, finish):
        product(spare, lambda cols, u: finish(cols, base[:, cols] + coef_c * u))

    def poly(src, spare, finish):
        product(src, lambda cols, u: linear(cols, base[:, cols], u, spare))
        quadratic(spare, finish)

    def keep(dst):
        def finish(cols, value):
            base[:, cols] = value
            dst[:, cols] = value.astype(jnp.bfloat16)

        return finish

    def first(cols, value):
        y = (factor * value).astype(jnp.bfloat16)
        left[:, cols] = y
        base[:, cols] = y.astype(jnp.float32)
        total[:, cols] = coef_a * y.astype(jnp.float32)

    def second(cols, value):
        keep(right)(cols, value)
        total[:, cols] += coef_b * value

    def third(cols, value):
        result = total[:, cols] + coef_c * value
        out_ref[:, cols] = (math.sqrt(max(D, F)) * result).astype(jnp.bfloat16)

    linear(slice(0, F), left[...].astype(jnp.float32), inverse * base[...], right)
    quadratic(right, first)
    poly(left, right, keep(left))
    product(left, keep(right))
    poly(right, left, second)
    poly(right, left, keep(right))
    product(right, keep(left))
    poly(left, right, third)

    for p in range(2):
        up_piece(last, 0, last, p).wait_send()
        down_piece(last, 4, last, p).wait_send()
    copy_sib(last).wait_send()


def body(grad, expert_ids):
    dma = pltpu.SemaphoreType.DMA
    bf16, f32 = jnp.bfloat16, jnp.float32
    out = pl.pallas_call(
        kernel,
        out_shape=jax.ShapeDtypeStruct((ROWS, F), bf16),
        in_specs=[pl.BlockSpec(memory_space=pl.ANY)] * 2,
        out_specs=pl.BlockSpec(memory_space=pltpu.VMEM),
        scratch_shapes=[
            pltpu.VMEM((ROWS, F), f32),
            pltpu.SMEM((TEAM,), jnp.int32),
            pltpu.SMEM((TEAM,), jnp.int32),
            pltpu.VMEM((GROUPS, GROUP, F), bf16),
            pltpu.VMEM((TEAM, GROUP, F), bf16),
            pltpu.VMEM((TEAM, GROUP, F), bf16),
            pltpu.VMEM((STEPS, 2 * GROUPS, GROUP, F), bf16),
            pltpu.VMEM((F, 2 * ROWS), bf16),
            pltpu.VMEM((F, F), f32),
            pltpu.VMEM((F, F), bf16),
            pltpu.VMEM((ROWS, F), f32),
            pltpu.VMEM((ROWS, F), f32),
            pltpu.VMEM((ROWS, F), bf16),
            pltpu.VMEM((ROWS, F), bf16),
            dma((4,)),
            dma,
            dma((2 * GROUPS,)),
            dma((TEAM,)),
            dma((TEAM,)),
            dma((2 * GROUPS,)),
            dma((2 * STEPS,)),
            dma((2 * STEPS,)),
            dma((2 * STEPS,)),
            dma((2 * STEPS,)),
            dma((STEPS,)),
            dma((STEPS,)),
        ],
        compiler_params=pltpu.CompilerParams(
            collective_id=0,
            has_side_effects=True,
            vmem_limit_bytes=55800000,
        ),
        cost_estimate=pl.CostEstimate(
            flops=2 * F * F * (D + 12 * ROWS), bytes_accessed=6 * ROWS * F, transcendentals=0
        ),
    )(grad.reshape(ROWS, F), expert_ids)
    return out.reshape(1, ROWS, F)


def solution(mesh):
    return jax.shard_map(
        body,
        mesh=mesh,
        in_specs=(P("expert", "dp", None), P()),
        out_specs=P("expert", "dp", None),
        check_vma=False,
    )
```

```python
import math

import jax
import jax.numpy as jnp
from jax import lax
from jax.experimental import pallas as pl
from jax.experimental.pallas import tpu as pltpu
from jax.sharding import PartitionSpec as P

D = 2048
F = 1408
ROWS = 128
GROUP = 16
GROUPS = 8
TEAM = 16
RING = 8
STEPS = 8

coef_a = 3.4445
coef_b = -4.775
coef_c = 2.0315
gram_eps = 1e-07

MESH = pl.DeviceIdType.MESH
SPLIT = [(0, 640), (640, 768)]
WIDE = [(0, F)]
PANELS = [(i, min(256, F - i)) for i in range(0, F, 256)]


def kernel(
    grad_ref,
    ids_ref,
    out_ref,
    raw,
    ids,
    holder,
    own,
    mid,
    stage,
    slots,
    turned,
    gram,
    amat,
    base,
    total,
    left,
    right,
    load_raw,
    load_ids,
    send1,
    recv1,
    send2,
    recv2,
    send_up,
    recv_up,
    send_down,
    recv_down,
    send_sib,
    recv_sib,
):
    dp = lax.axis_index("dp")
    me = lax.axis_index("expert")
    core = lax.rem(dp, 2)
    z = dp // 2
    sib = dp + 1 - 2 * core
    up = lax.rem(z + 1, RING) * 2 + core
    down = lax.rem(z + RING - 1, RING) * 2 + core

    def fetch_raw(q):
        rows = pl.ds(32 * q, 32)
        return pltpu.make_async_copy(grad_ref.at[rows], raw.at[rows], load_raw.at[q])

    fetch_ids = pltpu.make_async_copy(ids_ref, ids, load_ids)
    for q in range(4):
        fetch_raw(q).start()
    fetch_ids.start()
    barrier = pltpu.get_barrier_semaphore()

    @pl.loop(1, TEAM)
    def _(k):
        pl.semaphore_signal(
            barrier, inc=1, device_id=(dp, lax.rem(me + k, TEAM)), device_id_type=MESH
        )

    for other in (sib, up, down):
        pl.semaphore_signal(barrier, inc=1, device_id=(other, me), device_id_type=MESH)
    fetch_ids.wait()
    values = [ids[j] for j in range(TEAM)]
    for e in range(TEAM):
        slot = jnp.int32(0)
        for j in range(TEAM):
            slot = jnp.where(values[j] == e, j, slot)
        holder[e] = slot

    pl.semaphore_wait(barrier, TEAM + 2)

    def swap(row):
        return row // 2 + 2 * lax.rem(row, 2)

    def relay_of(wave, row, side):
        y = swap(row)
        return 4 * y + 2 * side + lax.rem(y + wave + core, 2)

    my_x, my_y = lax.rem(me, 4), me // 4
    my_group = 4 * lax.rem(my_x + my_y + core, 2) + swap(my_y)
    my_side = my_x // 2

    def piece(side):
        return pl.ds(*SPLIT[side])

    def copy1(wave, row, side):
        g = 4 * wave + row
        return pltpu.make_async_remote_copy(
            src_ref=own.at[g, :, piece(side)],
            dst_ref=mid.at[me, :, piece(side)],
            send_sem=send1.at[2 * g + side],
            recv_sem=recv1.at[me],
            device_id=(dp, relay_of(wave, row, side)),
            device_id_type=MESH,
        )

    def arrive1(s, side):
        return pltpu.make_async_remote_copy(
            src_ref=own.at[0, :, piece(side)],
            dst_ref=mid.at[s, :, piece(side)],
            send_sem=send1.at[0],
            recv_sem=recv1.at[s],
            device_id=(dp, s),
            device_id_type=MESH,
        )

    def copy2(e, side):
        return pltpu.make_async_remote_copy(
            src_ref=stage.at[e, :, piece(side)],
            dst_ref=slots.at[0, my_group, :, piece(side)],
            send_sem=send2.at[e],
            recv_sem=recv2.at[2 * my_group + side],
            device_id=(dp, e),
            device_id_type=MESH,
        )

    def arrive2(wave, row, side):
        g = 4 * wave + row
        return pltpu.make_async_remote_copy(
            src_ref=stage.at[0, :, piece(side)],
            dst_ref=slots.at[0, g, :, piece(side)],
            send_sem=send2.at[0],
            recv_sem=recv2.at[2 * g + side],
            device_id=(dp, relay_of(wave, row, side)),
            device_id_type=MESH,
        )

    for q in range(4):
        fetch_raw(q).wait()
        own[2 * q : 2 * q + 2] = (
            raw[32 * q : 32 * q + 32].reshape(2, GROUP, F).astype(jnp.bfloat16)
        )
        wave = q // 2

        @pl.loop(0, 2)
        def _(k):
            row = 2 * (q % 2) + lax.rem(k + me, 2)
            for side in range(2):

                @pl.when(relay_of(wave, row, side) != me)
                def _():
                    copy1(wave, row, side).start()

    for side in range(2):

        @pl.when(my_side == side)
        def _():
            mid[me, :, piece(side)] = own[my_group, :, piece(side)]

    for side in range(2):

        @pl.when(my_side == side)
        def _():
            @pl.loop(0, TEAM)
            def _(s):
                @pl.when(s != me)
                def _():
                    arrive1(s, side).wait_recv()

            for e in range(TEAM):
                stage[e, :, piece(side)] = mid[holder[e], :, piece(side)]

            @pl.loop(1, TEAM)
            def _(k):
                copy2(lax.rem(me + k, TEAM), side).start()

            slots[0, my_group, :, piece(side)] = stage[me, :, piece(side)]

    def part(first_group, count):
        return pl.ds(first_group, count)

    def up_piece(src, first_group, t, p):
        return pltpu.make_async_remote_copy(
            src_ref=slots.at[src, part(first_group + 2 * p, 2)],
            dst_ref=slots.at[t, part(2 * p, 2)],
            send_sem=send_up.at[2 * t + p],
            recv_sem=recv_up.at[2 * t + p],
            device_id=(up, me),
            device_id_type=MESH,
        )

    def down_piece(src, first_group, t, p):
        return pltpu.make_async_remote_copy(
            src_ref=slots.at[src, part(first_group + 2 * p, 2)],
            dst_ref=slots.at[t, part(4 + 2 * p, 2)],
            send_sem=send_down.at[2 * t + p],
            recv_sem=recv_down.at[2 * t + p],
            device_id=(down, me),
            device_id_type=MESH,
        )

    def copy_sib(t):
        return pltpu.make_async_remote_copy(
            src_ref=slots.at[t, part(0, GROUPS)],
            dst_ref=slots.at[t, part(GROUPS, GROUPS)],
            send_sem=send_sib.at[t],
            recv_sem=recv_sib.at[t],
            device_id=(sib, me),
            device_id_type=MESH,
        )

    for wave in range(2):
        for p in range(2):

            @pl.loop(2 * p, 2 * p + 2)
            def _(row):
                for side in range(2):

                    @pl.when(relay_of(wave, row, side) != me)
                    def _():
                        arrive2(wave, row, side).wait_recv()

            up_piece(0, 4 * wave, wave + 1, p).start()
            down_piece(0, 4 * wave, wave + 1, p).start()
    copy_sib(0).start()

    def turn(t, side):
        turned[:, side * ROWS : (side + 1) * ROWS] = (
            slots[t, side * GROUPS : (side + 1) * GROUPS].reshape(ROWS, F).T
        )

    def columns(t, start, size):
        return slots[t, :, :, start : start + size].reshape(2 * ROWS, size)

    def meet(t):
        turn(t, 0)
        copy_sib(t).wait_recv()
        turn(t, 1)

    gram[...] = jnp.zeros_like(gram)
    left[...] = slots[0, 0:GROUPS].reshape(ROWS, F)
    base[...] = left[...].astype(jnp.float32)

    @pl.loop(0, STEPS - 1)
    def _(k):
        t = k + 1

        @pl.when(t < STEPS - 1)
        def _():
            for p in range(2):
                up_piece(t, 0, t, p).wait_recv()

                @pl.when(t < STEPS - 2)
                def _():
                    up_piece(t, 0, t + 2, p).start()

                down_piece(t, 4, t, p).wait_recv()

                @pl.when(t < STEPS - 3)
                def _():
                    down_piece(t, 4, t + 2, p).start()

                @pl.when(t == STEPS - 2)
                def _():
                    down_piece(t, 4, t + 1, p).start()

            copy_sib(t).start()

        meet(k)
        for start, size in PANELS:
            end = start + size
            gram[0:end, start:end] += jnp.dot(
                turned[0:end, :], columns(k, start, size), preferred_element_type=jnp.float32
            )

    for wave in range(2):

        @pl.loop(0, 4)
        def _(row):
            for side in range(2):

                @pl.when(relay_of(wave, row, side) != me)
                def _():
                    copy1(wave, row, side).wait_send()

    for side in range(2):

        @pl.when(my_side == side)
        def _():
            @pl.loop(1, TEAM)
            def _(k):
                copy2(lax.rem(me + k, TEAM), side).wait_send()

    @pl.loop(1, STEPS - 1)
    def _(t):
        for p in range(2):
            up_piece(t, 0, t, p).wait_send()
            down_piece(t, 4, t, p).wait_send()

    @pl.loop(0, STEPS - 1)
    def _(t):
        copy_sib(t).wait_send()

    last = STEPS - 1
    for p in range(2):
        up_piece(last, 0, last, p).wait_recv()
        down_piece(last, 4, last, p).wait_recv()
    copy_sib(last).start()
    meet(last)
    squares = jnp.zeros((8, 128), jnp.float32)
    for start, size in PANELS:
        end = start + size
        panel = columns(last, start, size)
        for row, count in PANELS:
            if row > start:
                break
            rows = slice(row, row + count)
            g = gram[rows, start:end] + jnp.dot(
                turned[rows, :], panel, preferred_element_type=jnp.float32
            )
            amat[rows, start:end] = g.astype(jnp.bfloat16)
            folded = jnp.sum((g * g).reshape(count // 8, 8, size), axis=0)
            for lane in range(0, size, 128):
                lanes = folded[:, lane : lane + 128]
                squares = squares + (lanes if row == start else 2.0 * lanes)
        if start:
            amat[start:end, 0:start] = amat[0:start, start:end].T
    norm = jnp.sqrt(jnp.sum(squares, keepdims=True)) + gram_eps
    inverse = 1.0 / norm
    factor = 1.0 / jnp.sqrt(norm)

    def product(src, finish):
        for start, size in WIDE:
            cols = slice(start, start + size)
            finish(
                cols,
                inverse
                * jnp.dot(src[...], amat[:, cols], preferred_element_type=jnp.float32),
            )

    def linear(cols, x, u, spare):
        base[:, cols] = coef_a * x + coef_b * u
        spare[:, cols] = u.astype(jnp.bfloat16)

    def quadratic(spare, finish):
        product(spare, lambda cols, u: finish(cols, base[:, cols] + coef_c * u))

    def poly(src, spare, finish):
        product(src, lambda cols, u: linear(cols, base[:, cols], u, spare))
        quadratic(spare, finish)

    def keep(dst):
        def finish(cols, value):
            base[:, cols] = value
            dst[:, cols] = value.astype(jnp.bfloat16)

        return finish

    def first(cols, value):
        y = (factor * value).astype(jnp.bfloat16)
        left[:, cols] = y
        base[:, cols] = y.astype(jnp.float32)
        total[:, cols] = coef_a * y.astype(jnp.float32)

    def second(cols, value):
        keep(right)(cols, value)
        total[:, cols] += coef_b * value

    def third(cols, value):
        result = total[:, cols] + coef_c * value
        out_ref[:, cols] = (math.sqrt(max(D, F)) * result).astype(jnp.bfloat16)

    poly(left, right, first)
    poly(left, right, keep(left))
    product(left, keep(right))
    poly(right, left, second)
    poly(right, left, keep(right))
    product(right, keep(left))
    poly(left, right, third)

    for p in range(2):
        up_piece(last, 0, last, p).wait_send()
        down_piece(last, 4, last, p).wait_send()
    copy_sib(last).wait_send()


def body(grad, expert_ids):
    dma = pltpu.SemaphoreType.DMA
    bf16, f32 = jnp.bfloat16, jnp.float32
    out = pl.pallas_call(
        kernel,
        out_shape=jax.ShapeDtypeStruct((ROWS, F), bf16),
        in_specs=[pl.BlockSpec(memory_space=pl.ANY)] * 2,
        out_specs=pl.BlockSpec(memory_space=pltpu.VMEM),
        scratch_shapes=[
            pltpu.VMEM((ROWS, F), f32),
            pltpu.SMEM((TEAM,), jnp.int32),
            pltpu.SMEM((TEAM,), jnp.int32),
            pltpu.VMEM((GROUPS, GROUP, F), bf16),
            pltpu.VMEM((TEAM, GROUP, F), bf16),
            pltpu.VMEM((TEAM, GROUP, F), bf16),
            pltpu.VMEM((STEPS, 2 * GROUPS, GROUP, F), bf16),
            pltpu.VMEM((F, 2 * ROWS), bf16),
            pltpu.VMEM((F, F), f32),
            pltpu.VMEM((F, F), bf16),
            pltpu.VMEM((ROWS, F), f32),
            pltpu.VMEM((ROWS, F), f32),
            pltpu.VMEM((ROWS, F), bf16),
            pltpu.VMEM((ROWS, F), bf16),
            dma((4,)),
            dma,
            dma((2 * GROUPS,)),
            dma((TEAM,)),
            dma((TEAM,)),
            dma((2 * GROUPS,)),
            dma((2 * STEPS,)),
            dma((2 * STEPS,)),
            dma((2 * STEPS,)),
            dma((2 * STEPS,)),
            dma((STEPS,)),
            dma((STEPS,)),
        ],
        compiler_params=pltpu.CompilerParams(
            collective_id=0,
            has_side_effects=True,
            vmem_limit_bytes=55800000,
        ),
        cost_estimate=pl.CostEstimate(
            flops=2 * F * F * (D + 12 * ROWS), bytes_accessed=6 * ROWS * F, transcendentals=0
        ),
    )(grad.reshape(ROWS, F), expert_ids)
    return out.reshape(1, ROWS, F)


def solution(mesh):
    return jax.shard_map(
        body,
        mesh=mesh,
        in_specs=(P("expert", "dp", None), P()),
        out_specs=P("expert", "dp", None),
        check_vma=False,
    )
```
